32 devices in a mesh: dp: 16 (over z, y, x), tensor: 2 (over core).
Axes of the slice: x: 2, y: 2, z: 4, core: 2. Of those that a mesh axis runs over, the one named last changes fastest.
Arguments:
- tokens: bfloat16 [4096, 2048], P(('dp', 'tensor')), may hold values from -6 to 6
- segment_ids: int32 [4096], P('dp'), may hold values from 0 to 2, as said below
- ln1_gain: float32 [2048], replicated, may hold values from 0.5 to 1.5
- ln1_bias: float32 [2048], replicated, may hold values from -1.75 to 1.75
- qkv_weight: bfloat16 [3, 2048, 2048], P(None, 'dp', 'tensor'), may hold values from -0.125 to 0.125
- qkv_bias: float32 [3, 2048], P(None, 'tensor'), may hold values from -3 to 3
- out_weight: bfloat16 [2048, 2048], P('tensor', 'dp'), may hold values from -0.75 to 0.75
- ln2_gain: float32 [2048], replicated, may hold values from 0.5 to 1.5
- ln2_bias: float32 [2048], replicated, may hold values from -1.75 to 1.75
- gate_up_weight: bfloat16 [2, 2048, 5632], P(None, 'dp', 'tensor'), may hold values from -0.125 to 0.125
- down_weight: bfloat16 [5632, 2048], P('tensor', 'dp'), may hold values from -0.078125 to 0.078125
- out_grad: bfloat16 [4096, 2048], P(('dp', 'tensor')), may hold values from -12 to 12
Outputs:
- output: bfloat16 [4096, 2048], P(('dp', 'tensor'))
- tokens_grad: float32 [4096, 2048], P(('dp', 'tensor'))
- ln1_gain_grad: float32 [2048], replicated
- ln1_bias_grad: float32 [2048], replicated
- qkv_weight_grad: float32 [3, 2048, 2048], P(None, 'dp', 'tensor')
- qkv_bias_grad: float32 [3, 2048], replicated
- out_weight_grad: float32 [2048, 2048], P('tensor', 'dp')
- ln2_gain_grad: float32 [2048], replicated
- ln2_bias_grad: float32 [2048], replicated
- gate_up_weight_grad: float32 [2, 2048, 5632], P(None, 'dp', 'tensor')
- down_weight_grad: float32 [5632, 2048], P('tensor', 'dp')
The draws below stay inside these ranges and needn't reach their ends.
Inputs may be any that keep to these rules, and one draw needn't show every extreme that they name: `segment_ids`: numbers the documents of each sequence of 256 tokens 0, 1, ... in order; every sequence holds exactly 3 documents, and no document begins at the middle token (index 128) of its sequence.
All inputs are finite; a program needn't handle non-finite values.
Results may differ from the reference program's by a relative error of at most 0.014.
Values may be sent and summed in bfloat16 or wider, within the bound.
No kernel may reach another device: no remote copies, remote signals or barrier semaphores. Data moves between devices by JAX's collectives and lax.ppermute only.
A program may use at most 256 MiB of HBM per device.

```python
import jax
import jax.numpy as jnp
from jax import lax

D = 2048
FF = 5632
HD = 64
ROT = 16
DOCS = 3
SEQ = 256
HEADS = 32
SEQS = 16
TOKENS = 4096


def draw_segment_ids(key, part):
    key = jax.random.fold_in(key, 7)
    keys = jax.random.split(key, TOKENS // SEQ)

    def one_sequence(subkey):
        order = jax.random.permutation(subkey, SEQ - 2)
        picks = order[:DOCS - 1].astype(jnp.int32) + 1
        cuts = picks + (picks >= SEQ // 2).astype(jnp.int32)
        token_index = jnp.arange(SEQ, dtype=jnp.int32)
        return jnp.sum((token_index[:, None] >= cuts[None, :]).astype(jnp.int32), axis=1)
    return jax.vmap(one_sequence)(keys).reshape(TOKENS).astype(jnp.int32)


def with_spikes(values, rng, source, target, shards_of, factor):
    def block_of(dim):
        return (jnp.arange(values.shape[dim]) // (values.shape[dim] // shards_of)).reshape((-1,) + (1,) * (values.ndim - 1 - dim))

    one_side = jax.random.permutation(rng, shards_of)[block_of(target)]
    second = (block_of(target) + shards_of // 2) % shards_of
    return jnp.where((block_of(source) == one_side) | (block_of(source) == second), factor * values, values)


def levels(rng, extent, cuts, low, largest):
    def one(dim, parts):
        steps = jax.random.uniform(jax.random.fold_in(jax.random.fold_in(rng, 6), dim), (parts,), jnp.float32, low / len(cuts), largest / len(cuts))
        return jnp.repeat(jnp.exp(steps), extent[dim] // parts).reshape((-1,) + (1,) * (len(extent) - dim - 1))

    loudness = one(*cuts[0])
    for cut in cuts[1:]:
        loudness = loudness * one(*cut)
    return loudness


def scatter_about(stream_key, shape, deviation, limit, cuts=(), held_as=jnp.bfloat16):
    values = deviation * jax.random.normal(stream_key, shape, jnp.float32)
    if cuts:
        values = values * levels(stream_key, shape, cuts, -0.22, 0.18)
    return jnp.clip(values, -limit, limit).astype(held_as)


def noise_with(stream_key, dims, width, limit, cuts, heavy, held_as=jnp.bfloat16):
    values = width * jax.random.normal(stream_key, dims, jnp.float32)
    if cuts:
        values = values * levels(stream_key, dims, cuts, -0.22, 0.18)
    return jnp.clip(with_spikes(values, jax.random.fold_in(stream_key, 3), *heavy), -limit, limit).astype(held_as)


def setup_inputs(seed: int = 0) -> dict:
    seeds = jax.random.split(jax.random.key(seed), 13)
    tokens = scatter_about(seeds[0], (TOKENS, D), 1.0, 6.0, ((0, 32),))
    segment_ids = draw_segment_ids(jax.random.fold_in(seeds[12], 71), 0)
    ln1_gain = jnp.clip(1.0 + 0.1 * jax.random.normal(seeds[2], (D,), jnp.float32), 0.5, 1.5)
    ln1_bias = scatter_about(seeds[3], (D,), 0.3, 1.75, (), jnp.float32)
    qkv_weight = scatter_about(seeds[4], (3, D, D), D ** -0.5, 0.125, ((1, 16), (2, 2)))
    qkv_bias = scatter_about(seeds[5], (3, D), 0.5, 3.0, ((1, 2),), jnp.float32)
    out_weight = scatter_about(seeds[6], (D, D), (D // 32) ** -0.5, 0.75, ((0, 2), (1, 16)))
    ln2_gain = jnp.clip(1.0 + 0.1 * jax.random.normal(seeds[7], (D,), jnp.float32), 0.5, 1.5)
    ln2_bias = scatter_about(seeds[8], (D,), 0.3, 1.75, (), jnp.float32)
    gate_up_weight = scatter_about(seeds[9], (2, D, FF), D ** -0.5, 0.125, ((1, 16), (2, 2)))
    down_weight = scatter_about(seeds[10], (FF, D), FF ** -0.5, 0.078125, ((0, 2), (1, 16)))
    out_grad = noise_with(seeds[11], (TOKENS, D), 1.0, 12.0, ((0, 32),), (0, 1, 32, 2.75))
    return dict(tokens=tokens, segment_ids=segment_ids, ln1_gain=ln1_gain, ln1_bias=ln1_bias, qkv_weight=qkv_weight, qkv_bias=qkv_bias, out_weight=out_weight, ln2_gain=ln2_gain, ln2_bias=ln2_bias, gate_up_weight=gate_up_weight, down_weight=down_weight, out_grad=out_grad)


norm_eps = 1e-05
rope_base = 10000.0
score_scale = 0.125
masked_score = -1e+30

@jax.custom_vjp
def low(v):
    return lax.optimization_barrier(v.astype(jnp.bfloat16)).astype(jnp.float32)

@jax.custom_vjp
def low_back(v):
    return v

def low_keep(v):
    return (low(v), None)

def low_pass(kept, grad):
    return (grad,)

def back_keep(v):
    return (v, None)

def back_low(kept, grad):
    return (low(grad),)
low.defvjp(low_keep, low_pass)
low_back.defvjp(back_keep, back_low)

def doc_positions(segment):
    token_index = jnp.arange(segment.shape[0], dtype=jnp.int32)
    begins = jnp.concatenate([jnp.ones((1,), dtype=jnp.bool_), segment[1:] != segment[:-1]])
    starts = lax.cummax(jnp.where(begins, token_index, jnp.zeros_like(token_index)), axis=0)
    return token_index - starts

def rotary_tables(positions):
    half_rot = ROT // 2
    frequency = rope_base ** (-(2.0 * jnp.arange(half_rot, dtype=jnp.float32)) / ROT)
    angles = positions.astype(jnp.float32)[:, None] * frequency[None, :]
    return (jnp.cos(angles), jnp.sin(angles))

def rotate(heads_in, cosine, sine, turn_sign):
    half_rot = cosine.shape[-1]
    lead_half = heads_in[..., :half_rot]
    tail_half = heads_in[..., half_rot:2 * half_rot]
    remainder = heads_in[..., 2 * half_rot:]
    cos_b = cosine[:, None, :]
    sin_b = sine[:, None, :] * turn_sign
    return jnp.concatenate([lead_half * cos_b - tail_half * sin_b, tail_half * cos_b + lead_half * sin_b, remainder], axis=-1)

def layer_norm(values, gain, shift):
    row_mean = lax.optimization_barrier(jnp.mean(values, axis=-1, keepdims=True))
    centred = values - row_mean
    row_var = lax.optimization_barrier(jnp.mean(centred * centred, axis=-1, keepdims=True))
    return centred * lax.rsqrt(row_var + norm_eps) * gain + shift

def reference(tokens, segment_ids, ln1_gain, ln1_bias, qkv_weight, qkv_bias, out_weight, ln2_gain, ln2_bias, gate_up_weight, down_weight, out_grad):
    precise = lax.Precision.HIGHEST
    grouped = segment_ids.reshape(SEQS, SEQ)
    positions = jax.vmap(doc_positions)(grouped).reshape(TOKENS)
    cosine, sine = rotary_tables(positions)
    token_index = jnp.arange(SEQ, dtype=jnp.int32)
    causal = token_index[None, :] <= token_index[:, None]
    allowed = (grouped[:, :, None] == grouped[:, None, :]) & causal[None]

    def one_sequence(pieces):
        queries, keys_in, values, mask = pieces
        scores = low_back(jnp.einsum('qhd,khd->hqk', queries, keys_in, precision=precise) * score_scale)
        scores = jnp.where(mask[None], scores, masked_score)
        row_top = lax.optimization_barrier(jnp.max(scores, axis=-1, keepdims=True))
        weights = jnp.exp(scores - row_top)
        attn_probs = low(weights / lax.optimization_barrier(jnp.sum(weights, axis=-1, keepdims=True)))
        mixed = jnp.einsum('hqk,khd->qhd', attn_probs, values, precision=precise)
        return low(low_back(mixed))

    def forward(tokens_in, gain_one, shift_one, qkv_w, qkv_b, out_w, gain_two, shift_two, gate_up_w, down_w):
        h_one = low(layer_norm(tokens_in, gain_one, shift_one))
        lin = low_back(jnp.einsum('td,jdc->jtc', h_one, qkv_w, precision=precise) + qkv_b[:, None, :])
        shaped = lin.reshape(3, TOKENS, HEADS, HD)
        queries = low(rotate(shaped[0], cosine, sine, 1.0))
        keys_rot = low(rotate(shaped[1], cosine, sine, 1.0))
        values = low(shaped[2])
        mixed = lax.map(jax.checkpoint(one_sequence), (queries.reshape(SEQS, SEQ, HEADS, HD), keys_rot.reshape(SEQS, SEQ, HEADS, HD), values.reshape(SEQS, SEQ, HEADS, HD), allowed))
        mixed = mixed.reshape(TOKENS, D)
        attn_out = low_back(jnp.dot(mixed, out_w, precision=precise))
        resid_two = tokens_in + attn_out
        h_two = low(layer_norm(resid_two, gain_two, shift_two))
        gate_pre = low_back(jnp.dot(h_two, gate_up_w[0], precision=precise))
        up_values = low_back(jnp.dot(h_two, gate_up_w[1], precision=precise))
        hidden = low(jax.nn.silu(gate_pre) * up_values)
        mlp_out = low_back(jnp.dot(hidden, down_w, precision=precise))
        return resid_two + mlp_out
    floats = tuple((array.astype(jnp.float32) for array in (tokens, ln1_gain, ln1_bias, qkv_weight, qkv_bias, out_weight, ln2_gain, ln2_bias, gate_up_weight, down_weight)))
    result, pullback = jax.vjp(forward, *floats)
    grads = pullback(out_grad.astype(jnp.float32))
    return (result.astype(jnp.bfloat16), grads[0], grads[1], grads[2], grads[3], grads[4], grads[5], grads[6], grads[7], grads[8], grads[9])
```

```python
import jax
import jax.numpy as jnp
from jax import lax
from jax.sharding import PartitionSpec as P

HD = 64
ROT = 16

norm_eps = 1e-05
rope_base = 10000.0
score_scale = 0.125
masked_score = -1e30

GROUP_BITS = (1, 2)
BF = jnp.bfloat16
F32 = jnp.float32


def doc_positions(segment):
    token_index = jnp.arange(segment.shape[0], dtype=jnp.int32)
    begins = jnp.concatenate([jnp.ones((1,), dtype=jnp.bool_), segment[1:] != segment[:-1]])
    starts = lax.cummax(jnp.where(begins, token_index, jnp.zeros_like(token_index)), axis=0)
    return token_index - starts


def rotary_tables(positions):
    half_rot = ROT // 2
    frequency = rope_base ** (-(2.0 * jnp.arange(half_rot, dtype=F32)) / ROT)
    angles = positions.astype(F32)[:, None] * frequency[None, :]
    return (jnp.cos(angles), jnp.sin(angles))


def rotate(heads_in, cosine, sine, turn_sign):
    half_rot = cosine.shape[-1]
    lead_half = heads_in[..., :half_rot]
    tail_half = heads_in[..., half_rot : 2 * half_rot]
    remainder = heads_in[..., 2 * half_rot :]
    cos_b = cosine[:, None, :]
    sin_b = sine[:, None, :] * turn_sign
    return jnp.concatenate(
        [lead_half * cos_b - tail_half * sin_b, tail_half * cos_b + lead_half * sin_b, remainder],
        axis=-1,
    )


def norm_parts(values, gain, shift):
    row_mean = jnp.mean(values, axis=-1, keepdims=True)
    centred = values - row_mean
    inv_std = lax.rsqrt(jnp.mean(centred * centred, axis=-1, keepdims=True) + norm_eps)
    normed = centred * inv_std
    return (normed * gain + shift, normed, inv_std)


def norm_back(incoming, normed, inv_std, gain):
    scaled = incoming * gain
    adjusted = (
        scaled
        - jnp.mean(scaled, axis=-1, keepdims=True)
        - normed * jnp.mean(scaled * normed, axis=-1, keepdims=True)
    )
    return adjusted * inv_std


def attend(queries, keys_rot, values, allowed):
    scores = (
        jnp.einsum("qhd,khd->hqk", queries, keys_rot, preferred_element_type=F32) * score_scale
    )
    scores = jnp.where(allowed, scores, masked_score)
    row_top = jnp.max(scores, axis=-1, keepdims=True)
    weights = jnp.exp(scores - row_top)
    row_total = jnp.sum(weights, axis=-1, keepdims=True)
    attn_probs = (weights / row_total).astype(BF)
    mixed = jnp.einsum("hqk,khd->qhd", attn_probs, values, preferred_element_type=F32)
    return (mixed.astype(BF), row_top + jnp.log(row_total))


def attend_back(queries, keys_rot, values, log_total, mixed_grad, allowed):
    scores = (
        jnp.einsum("qhd,khd->hqk", queries, keys_rot, preferred_element_type=F32) * score_scale
    )
    scores = jnp.where(allowed, scores, masked_score)
    attn_probs = jnp.exp(scores - log_total)
    prob_grad = jnp.einsum("qhd,khd->hqk", mixed_grad, values, preferred_element_type=F32)
    value_grad = jnp.einsum(
        "hqk,qhd->khd", attn_probs.astype(BF), mixed_grad, preferred_element_type=F32
    )
    score_grad = (
        attn_probs * (prob_grad - jnp.sum(attn_probs * prob_grad, axis=-1, keepdims=True))
    ).astype(BF)
    query_grad = (
        jnp.einsum("hqk,khd->qhd", score_grad, keys_rot, preferred_element_type=F32) * score_scale
    )
    key_grad = (
        jnp.einsum("hqk,qhd->khd", score_grad, queries, preferred_element_type=F32) * score_scale
    )
    return (query_grad, key_grad, value_grad)


def dot(a, b, dims):
    return lax.dot_general(a, b, (dims, ((), ())), preferred_element_type=F32)


def on_device(
    tokens,
    segment_ids,
    ln1_gain,
    ln1_bias,
    qkv_weight,
    qkv_bias,
    out_weight,
    ln2_gain,
    ln2_bias,
    gate_up_weight,
    down_weight,
    out_grad,
):
    dp_size = lax.axis_size("dp")
    bits = dp_size.bit_length() - 1
    me = lax.axis_index("dp")
    core = lax.axis_index("tensor")
    rows, width = tokens.shape
    seq_len = segment_ids.shape[0]
    group = 1 << len(GROUP_BITS)
    far_bits = [b for b in reversed(range(bits)) if b not in GROUP_BITS]
    masks = [
        sum(1 << b for i, b in enumerate(GROUP_BITS) if (k >> i) & 1) for k in range(group)
    ]
    my_bit = [(me >> b) & 1 for b in range(bits)]
    rank = sum(my_bit[b] << i for i, b in enumerate(GROUP_BITS))
    heads = qkv_bias.shape[1] // HD // group
    head_cols = heads * HD
    hidden_cols = down_weight.shape[0] // group

    def swap(array, mask):
        if mask == 0:
            return array
        return lax.ppermute(array, "dp", [(d, d ^ mask) for d in range(dp_size)])

    def sibling(array):
        return lax.ppermute(array, "tensor", [(0, 1), (1, 0)])

    order = [bits - 1 - b for b in reversed(far_bits)]
    order += [bits - 1 - b for b in reversed(GROUP_BITS)]

    def to_rel(array):
        lead = array.ndim - 1
        cut = array.reshape(array.shape[:-1] + (2,) * bits + (width // dp_size,))
        cut = cut.transpose(list(range(lead)) + [lead + o for o in order] + [lead + bits])
        for i, b in enumerate(reversed(far_bits)):
            cut = jnp.where(my_bit[b] == 1, jnp.flip(cut, lead + i), cut)
        return cut.reshape(array.shape)

    def from_rel(array):
        lead = array.ndim - 1
        cut = array.reshape(array.shape[:-1] + (2,) * bits + (width // dp_size,))
        for i, b in enumerate(reversed(far_bits)):
            cut = jnp.where(my_bit[b] == 1, jnp.flip(cut, lead + i), cut)
        back = [order.index(i) for i in range(bits)]
        cut = cut.transpose(list(range(lead)) + [lead + o for o in back] + [lead + bits])
        return cut.reshape(array.shape)

    def natural(parts):
        cut = jnp.stack(parts)
        whole = cut.shape
        cut = cut.reshape((2,) * len(GROUP_BITS) + whole[1:])
        for i, b in enumerate(reversed(GROUP_BITS)):
            cut = jnp.where(my_bit[b] == 1, jnp.flip(cut, i), cut)
        return cut.reshape(whole)

    def to_group(pieces):
        return natural(
            [swap(lax.dynamic_index_in_dim(pieces, rank ^ k, 0, False), masks[k]) for k in range(group)]
        )

    def gather_rows(shard):
        for b in far_bits:
            shard = jnp.concatenate([shard, swap(shard, 1 << b)], axis=0)
        return shard

    def gather_cols(shard):
        for b in far_bits:
            shard = jnp.concatenate([shard, swap(shard, 1 << b)], axis=1)
        return shard

    def scatter_rows(grad):
        for b in reversed(far_bits):
            half = grad.shape[0] // 2
            grad = grad[:half] + swap(grad[half:].astype(BF), 1 << b).astype(F32)
        return grad

    def scatter_cols(grad):
        for b in reversed(far_bits):
            half = grad.shape[1] // 2
            grad = grad[:, :half] + swap(grad[:, half:].astype(BF), 1 << b).astype(F32)
        return grad

    def cut_cols(array, cols):
        return jnp.stack([array[:, i * cols : (i + 1) * cols] for i in range(group)])

    def spread(local):
        mine = jnp.stack([swap(local, m) for m in masks])
        return jnp.concatenate([mine, sibling(mine)], axis=1)

    def collect(blocks):
        both = blocks[:, :rows] + sibling(blocks[:, rows:].astype(BF)).astype(F32)
        total = both[0]
        for k in range(1, group):
            total = total + swap(both[k].astype(BF), masks[k]).astype(F32)
        return total

    block = width // dp_size

    q_cols = [cut_cols(qkv_weight[j], head_cols) for j in range(3)]
    w_qkv = gather_rows(to_group(jnp.concatenate(q_cols, axis=2)).reshape(group * block, -1))
    out_cut = to_group(out_weight.reshape(group, head_cols, block))
    w_out = gather_cols(out_cut.transpose(1, 0, 2).reshape(head_cols, group * block))
    g_cols = [cut_cols(gate_up_weight[j], hidden_cols) for j in range(2)]
    g_cut = jnp.concatenate(g_cols, axis=2)
    w_gate_up = gather_rows(to_group(g_cut).reshape(group * block, -1))
    d_cut = to_group(down_weight.reshape(group, hidden_cols, block))
    w_down = gather_cols(d_cut.transpose(1, 0, 2).reshape(hidden_cols, group * block))

    gains = to_rel(jnp.stack([ln1_gain, ln1_bias, ln2_gain, ln2_bias]))
    resid = to_rel(tokens).astype(F32)
    normed_in, normed_one, inv_one = norm_parts(resid, gains[0], gains[1])
    seq_in = spread(normed_in.astype(BF)).reshape(group * seq_len, width)
    grad_local = to_rel(out_grad)
    grad_rows = spread(grad_local).reshape(group * seq_len, width)

    positions = doc_positions(segment_ids)
    token_index = jnp.arange(seq_len, dtype=jnp.int32)
    facts = jnp.stack([segment_ids, positions, token_index])
    facts = jnp.stack([swap(facts, m) for m in masks])
    facts = jnp.where(core == 1, jnp.roll(facts, rows, axis=2), facts)
    segs, spots, index = facts[:, 0], facts[:, 1], facts[:, 2]
    allowed = (segs[:, :, None] == segs[:, None, :]) & (index[:, None, :] <= index[:, :, None])
    allowed = allowed[:, None]
    cosine, sine = rotary_tables(spots.reshape(-1))

    bias = lax.dynamic_slice_in_dim(qkv_bias, rank * head_cols, head_cols, 1).reshape(-1)
    projected = dot(seq_in, w_qkv, ((1,), (0,))) + bias
    shaped = projected.reshape(group * seq_len, 3, heads, HD)
    by_seq = (group, seq_len, heads, HD)
    queries = rotate(shaped[:, 0], cosine, sine, 1.0).astype(BF).reshape(by_seq)
    keys_rot = rotate(shaped[:, 1], cosine, sine, 1.0).astype(BF).reshape(by_seq)
    values = shaped[:, 2].astype(BF).reshape(by_seq)
    mixed, log_total = jax.vmap(attend)(queries, keys_rot, values, allowed)
    mixed_rows = mixed.reshape(group * seq_len, head_cols)
    attn_terms = dot(mixed_rows, w_out, ((1,), (0,)))
    resid_two = resid + collect(attn_terms.reshape(group, seq_len, width))
    normed_mid, normed_two, inv_two = norm_parts(resid_two, gains[2], gains[3])
    seq_mid = spread(normed_mid.astype(BF)).reshape(group * seq_len, width)

    gate_up = dot(seq_mid, w_gate_up, ((1,), (0,)))
    gate_pre = gate_up[:, :hidden_cols]
    up_values = gate_up[:, hidden_cols:]
    gate_sig = jax.nn.sigmoid(gate_pre)
    smooth = gate_pre * gate_sig
    hidden = (smooth * up_values).astype(BF)
    hidden_grad = dot(grad_rows, w_down, ((1,), (1,)))
    gate_grad = (hidden_grad * up_values * gate_sig * (1.0 + gate_pre * (1.0 - gate_sig))).astype(BF)
    up_grad = (hidden_grad * smooth).astype(BF)
    pair_grad = jnp.concatenate([gate_grad, up_grad], axis=1)
    mid_terms = dot(pair_grad, w_gate_up, ((1,), (1,)))
    mid_local = collect(mid_terms.reshape(group, seq_len, width))
    resid_grad = grad_local.astype(F32) + norm_back(mid_local, normed_two, inv_two, gains[2])
    attn_grad = spread(resid_grad.astype(BF)).reshape(group * seq_len, width)

    mlp_terms = dot(hidden, w_down, ((1,), (0,)))
    result = from_rel((resid_two + collect(mlp_terms.reshape(group, seq_len, width))).astype(BF))

    def final_rows(grad, parts):
        mine = scatter_rows(grad).reshape(group, block, -1)
        return to_group(mine.astype(BF)).reshape(group, block, parts, -1).transpose(2, 1, 0, 3).reshape(
            parts, block, -1
        ).astype(F32)

    def final_cols(grad):
        mine = scatter_cols(grad)
        mine = mine.reshape(grad.shape[0], group, block).transpose(1, 0, 2)
        return to_group(mine.astype(BF)).reshape(-1, block).astype(F32)

    down_grad = final_cols(dot(hidden, grad_rows, ((0,), (0,))))
    gate_up_grad = final_rows(dot(seq_mid, pair_grad, ((0,), (0,))), 2)

    mixed_grad = dot(attn_grad, w_out, ((1,), (1,))).astype(BF).reshape(by_seq)
    query_grad, key_grad, value_grad = jax.vmap(attend_back)(
        queries, keys_rot, values, log_total, mixed_grad, allowed
    )
    flat = (group * seq_len, heads, HD)
    lin_grad = jnp.stack(
        [
            rotate(query_grad.reshape(flat), cosine, sine, -1.0),
            rotate(key_grad.reshape(flat), cosine, sine, -1.0),
            value_grad.reshape(flat),
        ],
        axis=1,
    )
    lin_grad = lin_grad.reshape(group * seq_len, 3 * head_cols).astype(BF)
    qkv_grad = final_rows(dot(seq_in, lin_grad, ((0,), (0,))), 3)
    out_w_grad = final_cols(dot(mixed_rows, attn_grad, ((0,), (0,))))

    in_terms = dot(lin_grad, w_qkv, ((1,), (1,)))
    in_grad = collect(in_terms.reshape(group, seq_len, width))
    token_grad = from_rel(resid_grad + norm_back(in_grad, normed_one, inv_one, gains[0]))

    norm_sums = from_rel(
        jnp.stack(
            [
                jnp.sum(in_grad * normed_one, axis=0),
                jnp.sum(in_grad, axis=0),
                jnp.sum(mid_local * normed_two, axis=0),
                jnp.sum(mid_local, axis=0),
            ]
        )
    )
    bias_rows = jnp.sum(lin_grad.astype(F32), axis=0).reshape(3, head_cols)
    bias_full = lax.dynamic_update_slice(
        jnp.zeros((3, head_cols * group * lax.axis_size("tensor")), F32),
        bias_rows,
        (jnp.int32(0), (core * group + rank) * head_cols),
    )
    sums = jnp.concatenate([norm_sums.reshape(-1), bias_full.reshape(-1)])
    sums = sums + sibling(sums)
    for b in range(bits):
        sums = sums + swap(sums, 1 << b)
    norm_sums = sums[: 4 * width].reshape(4, width)
    return (
        result,
        token_grad,
        norm_sums[0],
        norm_sums[1],
        qkv_grad,
        sums[4 * width :].reshape(3, -1),
        out_w_grad,
        norm_sums[2],
        norm_sums[3],
        gate_up_grad,
        down_grad,
    )


def solution(mesh):
    return jax.shard_map(
        on_device,
        mesh=mesh,
        in_specs=(
            P(("dp", "tensor"), None),
            P("dp"),
            P(),
            P(),
            P(None, "dp", "tensor"),
            P(None, "tensor"),
            P("tensor", "dp"),
            P(),
            P(),
            P(None, "dp", "tensor"),
            P("tensor", "dp"),
            P(("dp", "tensor"), None),
        ),
        out_specs=(
            P(("dp", "tensor"), None),
            P(("dp", "tensor"), None),
            P(),
            P(),
            P(None, "dp", "tensor"),
            P(),
            P("tensor", "dp"),
            P(),
            P(),
            P(None, "dp", "tensor"),
            P("tensor", "dp"),
        ),
        check_vma=False,
    )
```

```python
import functools

import jax
import jax.numpy as jnp
from jax import lax
from jax.experimental import pallas as pl
from jax.experimental.pallas import tpu as pltpu
from jax.sharding import PartitionSpec as P

HD = 64
ROT = 16
LANES = 128

norm_eps = 1e-05
rope_base = 10000.0
score_scale = 0.125
masked_score = -1e30

GROUP_BITS = (1, 2)
BF = jnp.bfloat16
F32 = jnp.float32
COST = 30
VMEM_LIMIT = 60 * 1024 * 1024


def doc_positions(segment):
    token_index = jnp.arange(segment.shape[0], dtype=jnp.int32)
    begins = jnp.concatenate([jnp.ones((1,), dtype=jnp.bool_), segment[1:] != segment[:-1]])
    starts = lax.cummax(jnp.where(begins, token_index, jnp.zeros_like(token_index)), axis=0)
    return token_index - starts


def norm_parts(values, gain, shift):
    row_mean = jnp.mean(values, axis=-1, keepdims=True)
    centred = values - row_mean
    inv_std = lax.rsqrt(jnp.mean(centred * centred, axis=-1, keepdims=True) + norm_eps)
    normed = centred * inv_std
    return (normed * gain + shift, normed, inv_std)


def norm_back(incoming, normed, inv_std, gain):
    scaled = incoming * gain
    adjusted = (
        scaled
        - jnp.mean(scaled, axis=-1, keepdims=True)
        - normed * jnp.mean(scaled * normed, axis=-1, keepdims=True)
    )
    return adjusted * inv_std


def dot(a, b, a_dim, b_dim):
    return lax.dot_general(
        a, b, (((a_dim,), (b_dim,)), ((), ())), preferred_element_type=F32
    )


def whole(shape, once=False):
    zeros = (0,) * len(shape)
    return pl.BlockSpec(
        shape, lambda *_: zeros, pipeline_mode=pl.Buffered(buffer_count=1) if once else None
    )


def each(shape):
    zeros = (0,) * (len(shape) - 1)
    return pl.BlockSpec((None,) + shape[1:], lambda k, *_: (k,) + zeros)


def call(kernel, ins, out_shapes, flops, in_specs=None, out_specs=None, grid=(1,), scratch=()):
    moved = sum(v.size * v.dtype.itemsize for v in ins)
    moved += sum(s.size * s.dtype.itemsize for s in out_shapes)
    return pl.pallas_call(
        kernel,
        grid=grid,
        in_specs=in_specs or [whole(v.shape) for v in ins],
        out_specs=out_specs or [whole(s.shape) for s in out_shapes],
        out_shape=list(out_shapes),
        scratch_shapes=list(scratch),
        compiler_params=pltpu.CompilerParams(vmem_limit_bytes=VMEM_LIMIT),
        cost_estimate=pl.CostEstimate(flops=COST * flops, bytes_accessed=COST * moved, transcendentals=0),
    )(*ins)


def shaped(shape, dtype):
    return jax.ShapeDtypeStruct(shape, dtype)


def deal(cols, group):
    full = cols // (LANES * group) * LANES
    share = (cols - full * group) // group
    return full, share


def pack_attn_kernel(group, qkv_ref, out_ref, sent_ref):
    cols = qkv_ref.shape[2] // group
    block = qkv_ref.shape[1]
    for k in range(group):
        at, here = slice(k * cols, (k + 1) * cols), slice(k * block, (k + 1) * block)
        for j in range(3):
            sent_ref[here, j * cols : (j + 1) * cols] = qkv_ref[j, :, at]
        sent_ref[here, 3 * cols :] = out_ref[at, :].T


TILE = 2 * LANES


def column(j, at):
    return at // TILE * 3 * TILE + j * TILE + at % TILE


def pack_mlp_kernel(group, gate_up_ref, down_ref, sent_ref):
    full, share = deal(gate_up_ref.shape[2], group)
    block = gate_up_ref.shape[1]
    per = LANES // share
    lane = lax.broadcasted_iota(jnp.int32, (1, LANES), 1) // share
    for k in range(group):
        here = slice(k * block, (k + 1) * block)
        for at in range(0, full + LANES, LANES):
            own = at < full
            start = k * full + at if own else group * full + k // per * LANES
            take = slice(start, start + LANES)
            for j in range(3):
                value = gate_up_ref[j, :, take] if j < 2 else down_ref[take, :].T
                if not own:
                    value = jnp.where(lane == k % per, value, 0).astype(BF)
                to = column(j, at)
                sent_ref[here, to : to + LANES] = value


def finish_mlp_kernel(group, *refs):
    got, (gate_up_ref, down_ref) = refs[:-2], refs[-2:]
    full, share = deal(gate_up_ref.shape[2], group)
    block = gate_up_ref.shape[1]
    per = LANES // share

    def taken(k, j, at):
        to = column(j, at % TILE)
        return got[at // TILE][k * block : (k + 1) * block, to : to + LANES].astype(F32)

    for j in range(3):
        for at in range(0, full + LANES, LANES):
            own = at < full
            for k in range(0, group, 1 if own else per):
                start = k * full + at if own else group * full + k // per * LANES
                take = slice(start, start + LANES)
                value = sum(taken(k + i, j, at) for i in range(1 if own else per))
                if j < 2:
                    gate_up_ref[j, :, take] = value
                else:
                    down_ref[take, :] = value.T


def finish_attn_kernel(group, got_ref, qkv_ref, out_ref):
    cols = qkv_ref.shape[2] // group
    block = qkv_ref.shape[1]
    for k in range(group):
        here, at = slice(k * block, (k + 1) * block), slice(k * cols, (k + 1) * cols)
        for j in range(3):
            qkv_ref[j, :, at] = got_ref[here, j * cols : (j + 1) * cols].astype(F32)
        out_ref[at, :] = got_ref[here, 3 * cols :].astype(F32).T


def spans(weights):
    at = 0
    for w in weights:
        yield slice(at, at + w.shape[0]), w
        at += w.shape[0]


def turn(value, tables, sign):
    cosine, lead, tail = tables
    ahead = pltpu.roll(value, LANES - ROT // 2, 1)
    behind = pltpu.roll(value, ROT // 2, 1)
    return value * cosine + (ahead * lead + behind * tail) * sign


def soft(queries, keys, mask):
    scores = dot(queries, keys, 1, 1) * score_scale + mask
    weights = jnp.exp(scores - jnp.max(scores, axis=-1, keepdims=True))
    return weights * (1.0 / jnp.sum(weights, axis=-1, keepdims=True))


def own_head(half):
    return lax.broadcasted_iota(jnp.int32, (1, LANES), 1) // HD == half


def attend_kernel(far, own_ref, sib_ref, bias_ref, mask_ref, cos_ref, lead_ref, tail_ref, *refs):
    weights, refs = refs[:far], refs[far:]
    qkv_ref, mixed_own, mixed_sib, mine_ref, other_ref, lines, mixed_ref = refs
    rows = mine_ref.shape[0]
    lines[:rows] = own_ref[:rows]
    lines[rows:] = sib_ref[:rows]
    cols = mixed_ref.shape[1]
    tables = (cos_ref[...], lead_ref[...], tail_ref[...])
    lin = bias_ref[...]
    for at, w in spans(weights):
        lin = lin + dot(lines[:, at], w[:, : 3 * cols], 1, 0)
    mask = mask_ref[...]
    for i in range(cols // LANES):
        at = [slice(j * cols + i * LANES, j * cols + (i + 1) * LANES) for j in range(3)]
        queries = turn(lin[:, at[0]], tables, 1.0).astype(BF)
        keys = turn(lin[:, at[1]], tables, 1.0).astype(BF)
        values = lin[:, at[2]].astype(BF)
        qkv_ref[:, at[0]] = queries
        qkv_ref[:, at[1]] = keys
        qkv_ref[:, at[2]] = values
        mixed = None
        for half in range(LANES // HD):
            here = own_head(half)
            probs = soft(jnp.where(here, queries, 0).astype(BF), keys, mask).astype(BF)
            part = dot(probs, values, 1, 0)
            mixed = part if mixed is None else jnp.where(here, part, mixed)
        mixed_ref[:, i * LANES : (i + 1) * LANES] = mixed.astype(BF)
    mixed_own[...] = mixed_ref[:rows]
    mixed_sib[...] = mixed_ref[rows:]
    for at, w in spans(weights):
        term = dot(mixed_ref[...], w[:, 3 * cols :], 1, 1)
        mine_ref[:, at] = term[:rows]
        other_ref[:, at] = term[rows:].astype(BF)


def attend_back_kernel(far, own_ref, sib_ref, qkv_ref, mask_ref, cos_ref, lead_ref, tail_ref, *refs):
    weights, refs = refs[:far], refs[far:]
    lin_own, lin_sib, sums_ref, mine_ref, other_ref, lines, lin_ref = refs
    rows = own_ref.shape[0]
    lines[:rows] = own_ref[...]
    lines[rows:] = sib_ref[...]
    cols = qkv_ref.shape[1] // 3
    tables = (cos_ref[...], lead_ref[...], tail_ref[...])
    mixed_grad = sum(dot(lines[:, at], w[:, 3 * cols :], 1, 0) for at, w in spans(weights))
    mixed_grad = mixed_grad.astype(BF)
    mask = mask_ref[...]
    for i in range(cols // LANES):
        at = [slice(j * cols + i * LANES, j * cols + (i + 1) * LANES) for j in range(3)]
        queries, keys, values = (qkv_ref[:, a] for a in at)
        grad = mixed_grad[:, i * LANES : (i + 1) * LANES]
        found = [None] * 3
        for half in range(LANES // HD):
            here = own_head(half)
            probs = soft(jnp.where(here, queries, 0).astype(BF), keys, mask)
            value_grad = dot(probs.astype(BF), grad, 0, 0)
            prob_grad = dot(jnp.where(here, grad, 0).astype(BF), values, 1, 1)
            score_grad = (
                probs * (prob_grad - jnp.sum(probs * prob_grad, axis=-1, keepdims=True))
            ).astype(BF)
            query_grad = dot(score_grad, keys, 1, 0)
            key_grad = dot(score_grad, queries, 0, 0)
            parts = (query_grad, key_grad, value_grad)
            found = [p if f is None else jnp.where(here, p, f) for p, f in zip(parts, found)]
        lin_ref[:, at[0]] = turn(found[0] * score_scale, tables, -1.0).astype(BF)
        lin_ref[:, at[1]] = turn(found[1] * score_scale, tables, -1.0).astype(BF)
        lin_ref[:, at[2]] = found[2].astype(BF)
    lin_own[...] = lin_ref[:rows]
    lin_sib[...] = lin_ref[rows:]
    sums_ref[...] = jnp.sum(lin_ref[...].astype(F32), axis=0, keepdims=True)
    for at, w in spans(weights):
        term = dot(lin_ref[...], w[:, : 3 * cols], 1, 1)
        mine_ref[:, at] = term[:rows]
        other_ref[:, at] = term[rows:].astype(BF)


def mlp_kernel(far, tiles, first, *refs):
    lines, grads, refs = refs[:2], refs[2:4], refs[4:]
    before, refs = (None, refs) if first else (refs[:2], refs[2:])
    weights, refs = refs[: far * tiles], refs[far * tiles :]
    found, sums, (held, held_grad) = refs[: 4 * tiles], refs[-4:-2], refs[-2:]
    rows = lines[0].shape[0]
    for half in range(2):
        here = slice(half * rows, (half + 1) * rows)
        held[here] = lines[half][...]
        held_grad[here] = grads[half][...]
    inner = []
    for t in range(tiles):
        mine = weights[t * far : (t + 1) * far]
        gate_up = sum(dot(held[:, at], w[:, : 2 * TILE], 1, 0) for at, w in spans(mine))
        hidden_grad = sum(dot(held_grad[:, at], w[:, 2 * TILE :], 1, 0) for at, w in spans(mine))
        gate_pre, up_values = gate_up[:, :TILE], gate_up[:, TILE:]
        gate_sig = jax.nn.sigmoid(gate_pre)
        smooth = gate_pre * gate_sig
        gate_grad = hidden_grad * up_values * gate_sig * (1.0 + gate_pre * (1.0 - gate_sig))
        hidden = (smooth * up_values).astype(BF)
        pair = jnp.concatenate([gate_grad.astype(BF), (hidden_grad * smooth).astype(BF)], axis=1)
        for half in range(2):
            here = slice(half * rows, (half + 1) * rows)
            found[4 * t + half][...] = pair[here]
            found[4 * t + 2 + half][...] = hidden[here]
        inner.append(pair)
    for p, (at, _) in enumerate(spans(weights[:far])):
        term = sum(
            dot(pair, weights[t * far + p][:, : 2 * TILE], 1, 1) for t, pair in enumerate(inner)
        )
        for half in range(2):
            part = term[half * rows : (half + 1) * rows]
            if not first:
                part = part + before[half][:, at]
            sums[half][:, at] = part.astype(sums[half].dtype)


def mlp_out_kernel(far, tiles, *refs):
    hiddens, refs = refs[: 2 * tiles], refs[2 * tiles :]
    weights, outs = refs[: far * tiles], refs[far * tiles :]
    for half in range(2):
        for p, (at, _) in enumerate(spans(weights[:far])):
            term = sum(
                dot(hiddens[2 * t + half][...], weights[t * far + p][...], 1, 1)
                for t in range(tiles)
            )
            outs[half][:, at] = term.astype(outs[half].dtype)


def grad_kernel(kinds, adds, *refs):
    lefts, rights = [], []
    at = 0
    for count in kinds:
        lefts.append(refs[at : at + 2])
        rights.append([refs[at + 2 + 2 * c : at + 4 + 2 * c] for c in range(count)])
        at += 2 + 2 * count
    more = refs[at : at + sum(adds)]
    outs = refs[at + sum(adds) :]
    start = 0
    for left, columns in zip(lefts, rights):
        for right in columns:
            size = right[0].shape[1]
            here = slice(start, start + size)
            start += size
            total = sum(dot(a[...], b[...], 0, 0) for a, b in zip(left, right))
            parts = len(adds)
            depth = total.shape[0] // parts
            used = 0
            for i, count in enumerate(adds):
                part = total[i * depth : (i + 1) * depth]
                for extra in more[used : used + count]:
                    part = part + extra[:, here].astype(F32)
                used += count
                out = outs[i] if len(outs) > 1 else outs[0]
                lines = slice(None) if len(outs) > 1 else slice(i * depth, (i + 1) * depth)
                out[lines, here] = part.astype(BF)


def on_device(
    tokens,
    segment_ids,
    ln1_gain,
    ln1_bias,
    qkv_weight,
    qkv_bias,
    out_weight,
    ln2_gain,
    ln2_bias,
    gate_up_weight,
    down_weight,
    out_grad,
):
    dp_size = lax.axis_size("dp")
    bits = dp_size.bit_length() - 1
    me = lax.axis_index("dp")
    core = lax.axis_index("tensor")
    rows, width = tokens.shape
    seq_len = segment_ids.shape[0]
    group = 1 << len(GROUP_BITS)
    far_bits = [b for b in reversed(range(bits)) if b not in GROUP_BITS]
    my_bit = [(me >> b) & 1 for b in range(bits)]
    rank = sum(my_bit[b] << i for i, b in enumerate(GROUP_BITS))
    heads = qkv_bias.shape[1] // HD // group
    head_cols = heads * HD
    hidden_cols = deal(down_weight.shape[0], group)[0] + LANES

    def swap(array, mask):
        if mask == 0:
            return array
        return lax.ppermute(array, "dp", [(d, d ^ mask) for d in range(dp_size)])

    def sibling(array):
        return lax.ppermute(array, "tensor", [(0, 1), (1, 0)])

    order = [bits - 1 - b for b in reversed(far_bits)]
    order += [bits - 1 - b for b in reversed(GROUP_BITS)]

    def to_rel(array):
        lead = array.ndim - 1
        cut = array.reshape(array.shape[:-1] + (2,) * bits + (width // dp_size,))
        cut = cut.transpose(list(range(lead)) + [lead + o for o in order] + [lead + bits])
        for i, b in enumerate(reversed(far_bits)):
            cut = jnp.where(my_bit[b] == 1, jnp.flip(cut, lead + i), cut)
        return cut.reshape(array.shape)

    def from_rel(array):
        lead = array.ndim - 1
        cut = array.reshape(array.shape[:-1] + (2,) * bits + (width // dp_size,))
        for i, b in enumerate(reversed(far_bits)):
            cut = jnp.where(my_bit[b] == 1, jnp.flip(cut, lead + i), cut)
        back = [order.index(i) for i in range(bits)]
        cut = cut.transpose(list(range(lead)) + [lead + o for o in back] + [lead + bits])
        return cut.reshape(array.shape)

    block = width // dp_size
    shard_rows = group * block
    far = 1 << len(far_bits)
    bands = [
        [d for d in range(dp_size) if all((d ^ first) >> b & 1 == 0 for b in far_bits)]
        for first in range(dp_size)
        if all(first >> b & 1 == 0 for b in GROUP_BITS)
    ]

    def exchange(rows_by_rank):
        return lax.all_to_all(rows_by_rank, "dp", 0, 0, axis_index_groups=bands, tiled=True)

    def tie(value, *after):
        return lax.optimization_barrier((value, *after))[0]

    def pack(kernel, ins, cols):
        return call(
            functools.partial(kernel, group), ins, [shaped((shard_rows, cols), BF)], 0
        )[0]

    def gather(shard, subs, after=()):
        depth = shard_rows // subs
        parts = [tie(shard[i * depth : (i + 1) * depth], *after) for i in range(subs)]
        pieces = [parts]
        for n, b in enumerate(far_bits):
            came = [[swap(p, 1 << b) for p in piece] for piece in pieces[1:]]
            whole_shard = n > 0 and len(pieces) > 1
            first = [swap(shard, 1 << b)] if whole_shard else [swap(p, 1 << b) for p in parts]
            pieces = pieces + [first] + came
        return pieces

    def flat(pieces, shard):
        return [shard] + [p for piece in pieces[1:] for p in piece]

    def spread(local, after=(), then=()):
        mine = exchange(tie(jnp.broadcast_to(local, (group,) + local.shape), *after))
        return mine, sibling(tie(mine, *then))

    def half(array):
        return array.reshape((-1,) + array.shape[2:])

    def by_block(array):
        return array.reshape((group, -1) + array.shape[1:])

    def collect(mine, other, after=(), then=()):
        other = sibling(tie(other, *after))
        both = (by_block(mine) + by_block(other).astype(F32)).astype(BF)
        return jnp.sum(exchange(tie(both, *then)).astype(F32), axis=0)

    def arrived(pieces):
        return [p for piece in pieces for p in piece]

    def weight_grads(kinds, subs):
        cols = sum(c[0].shape[1] for _, sets in kinds for c in sets)
        spec = lambda v, i: pl.BlockSpec((v.shape[0], shard_rows), lambda *_: (0, i))

        def make(i, adds, outs, after):
            ins, specs = [], []
            for left, sets in kinds:
                ins += left
                specs += [spec(v, i) for v in left]
                for s in sets:
                    ins += s
                    specs += [whole(v.shape) for v in s]
            counts = [len(a) for a in adds]
            for a in adds:
                ins += a
                specs += [whole(v.shape) for v in a]
            ins[0] = tie(ins[0], *after)
            return call(
                functools.partial(grad_kernel, [len(s) for _, s in kinds], counts),
                ins,
                [shaped((shard_rows // outs, cols), BF)] * outs,
                2 * group * seq_len * shard_rows * cols,
                in_specs=specs,
            )

        adds = [[[] for _ in range(subs)] for _ in range(far)]
        count = far
        after = ()
        for b in reversed(far_bits):
            count //= 2
            for i in reversed(range(count)):
                parts = make(i + count, adds[i + count], subs, after)
                came = [swap(p, 1 << b) for p in parts]
                for j in range(subs):
                    adds[i][j].append(came[j])
                after = (yield list(parts), came) or ()
        yield make(0, adds[0], 1, after), None

    def finish(kernel, came, shapes):
        return call(functools.partial(kernel, group), came, [shaped(s, F32) for s in shapes], 0)

    gains = to_rel(jnp.stack([ln1_gain, ln1_bias, ln2_gain, ln2_bias]))
    resid = to_rel(tokens).astype(F32)
    normed_in, normed_one, inv_one = norm_parts(resid, gains[0], gains[1])
    note = jnp.pad(segment_ids.astype(BF)[None], ((0, 15), (0, width - seq_len)))
    message = jnp.concatenate([normed_in.astype(BF), note], axis=0)

    attn_pack = pack(pack_attn_kernel, [qkv_weight, out_weight], 4 * head_cols)
    attn_shard = exchange(attn_pack)
    mlp_pack = pack(pack_mlp_kernel, [tie(gate_up_weight, attn_shard), down_weight], 3 * hidden_cols)
    mlp_shard = exchange(tie(mlp_pack, attn_shard))
    attn_pieces = gather(attn_shard, 1)
    w_attn = flat(attn_pieces, attn_shard)
    heard = spread(message, [mlp_shard] + attn_pieces[1], w_attn[1:])
    tiles = hidden_cols // TILE
    mlp_pieces = []
    after = attn_pieces[1]
    for t in range(tiles):
        shard = tie(mlp_shard[:, t * 3 * TILE : (t + 1) * 3 * TILE], *after)
        mlp_pieces.append(gather(shard, 1))
        after = mlp_pieces[t][1]
    w_mlp = [flat(pieces, pieces[0][0]) for pieces in mlp_pieces]
    grad_local = to_rel(out_grad)
    grad_rows = spread(grad_local, [heard[0]])

    segs = heard[0][:, rows, :seq_len].astype(jnp.int32)
    seq_in = [half(h[:, :rows]) for h in heard]
    spots = jax.vmap(doc_positions)(segs)
    segs, spots = (jnp.where(core == 1, jnp.roll(v, rows, axis=1), v) for v in (segs, spots))
    index = jnp.arange(seq_len, dtype=jnp.int32)
    index = jnp.where(core == 1, jnp.roll(index, rows), index)
    allowed = (segs[:, :, None] == segs[:, None, :]) & (index[None, :] <= index[:, None])
    mask = jnp.where(allowed, 0.0, masked_score).astype(F32)
    dim = jnp.arange(LANES, dtype=jnp.int32) % HD
    pair = (dim % (ROT // 2)).astype(F32)
    speed = jnp.where(dim < ROT, rope_base ** (-2.0 * pair / ROT), 0.0)
    angles = spots.astype(F32)[..., None] * speed
    cosine, sine = jnp.cos(angles), jnp.sin(angles)
    lead = jnp.where(dim < ROT // 2, -sine, 0.0)
    tail = jnp.where((dim >= ROT // 2) & (dim < ROT), sine, 0.0)

    bias = lax.dynamic_slice_in_dim(qkv_bias, rank * head_cols, head_cols, 1).reshape(1, -1)
    facts = [mask, cosine, lead, tail]
    lines = pltpu.VMEM((seq_len, width), BF)
    mine, other = shaped((group * rows, width), F32), shaped((group * rows, width), BF)
    mine3, other3 = (shaped((group, rows, width), t) for t in (F32, BF))
    qkv_shape = shaped((group, seq_len, 3 * head_cols), BF)
    mixed_shape = shaped((group, rows, head_cols), BF)
    lin_shape = shaped((group, rows, 3 * head_cols), BF)
    attn_flops = 2 * group * seq_len * width * 4 * head_cols

    ins = [tie(heard[0], *mlp_pieces[0][1]), heard[1], bias] + facts + w_attn
    outs = [qkv_shape, mixed_shape, mixed_shape, mine3, other3]
    qkv, mixed_own, mixed_sib, *terms = call(
        functools.partial(attend_kernel, len(w_attn)),
        ins,
        outs,
        attn_flops,
        in_specs=[each(v.shape) for v in heard]
        + [whole(bias.shape)]
        + [each(v.shape) for v in facts]
        + [whole(v.shape) for v in w_attn],
        out_specs=[each(v.shape) for v in outs],
        grid=(group,),
        scratch=[lines, pltpu.VMEM((seq_len, head_cols), BF)],
    )
    mixed = [half(mixed_own), half(mixed_sib)]
    attn_sum = collect(*map(half, terms), mlp_pieces[0][2], [grad_rows[0]])
    early = arrived(mlp_pieces[0][3:]) + [p for pieces in mlp_pieces[1:2] for p in arrived(pieces[1:3])]
    resid_two = resid + tie(attn_sum, *early)
    normed_mid, normed_two, inv_two = norm_parts(resid_two, gains[2], gains[3])
    late = [p for pieces in mlp_pieces[1:2] for p in arrived(pieces[3:])]
    late += [p for pieces in mlp_pieces[2:] for p in arrived(pieces[1:3])]
    seq_mid = [half(h) for h in spread(normed_mid.astype(BF), (), late)]
    grad_rows = [half(h) for h in grad_rows]

    row_spec = pl.BlockSpec((rows, width), lambda k: (k, 0))
    pair_spec, hidden_spec = (pl.BlockSpec((rows, n * TILE), lambda k: (k, 0)) for n in (2, 1))
    pair_shape, hidden_shape = (shaped((group * rows, n * TILE), BF) for n in (2, 1))
    pairs, hiddens, mlp_steps, mid = [], [], [], []
    parts, came = [], []
    for batch in (range(tiles - 1), range(tiles - 1, tiles)):
        ins = [tie(seq_mid[0], *parts), seq_mid[1], *grad_rows] + mid
        final = batch[-1] == tiles - 1
        weights = [w for t in batch for w in w_mlp[t]]
        *inner, mid_own, mid_sib = call(
            functools.partial(mlp_kernel, far, len(batch), not mid),
            ins + weights,
            ([pair_shape] * 2 + [hidden_shape] * 2) * len(batch) + [mine, other if final else mine],
            10 * group * seq_len * width * TILE * len(batch),
            in_specs=[row_spec] * len(ins) + [whole(w.shape) for w in weights],
            out_specs=([pair_spec] * 2 + [hidden_spec] * 2) * len(batch) + [row_spec] * 2,
            grid=(group,),
            scratch=[lines, lines],
        )
        mid = [mid_own, mid_sib]
        for n, t in enumerate(batch):
            pairs.append(inner[4 * n : 4 * n + 2])
            hiddens.append(inner[4 * n + 2 : 4 * n + 4])
            mlp_steps.append(weight_grads([(seq_mid, [pairs[t]]), (grad_rows, [hiddens[t]])], 1))
            more, came_here = next(mlp_steps[t])
            parts = parts + more
            came.append(came_here)
    came_two = []
    for steps in mlp_steps:
        more, came_here = steps.send(parts)
        parts = parts + more
        came_two.append(came_here)
    mid_local = tie(collect(mid_own, mid_sib, (), came[0]), *parts, *came[1])
    resid_grad = grad_local.astype(F32) + norm_back(mid_local, normed_two, inv_two, gains[2])
    resid_back = resid_grad.astype(BF)
    firsts = [steps.send([resid_back])[0] for steps in mlp_steps]
    attn_grad = spread(resid_back, (), [p for f in firsts[:2] for p in f])

    parts = [p for f in firsts for p in f] + came_two[0]
    out_ins = [h for pair in hiddens for h in pair]
    out_ins[0] = tie(out_ins[0], resid_back)
    out_terms = call(
        functools.partial(mlp_out_kernel, far, tiles),
        out_ins + [w for ws in w_mlp for w in ws],
        [mine, other],
        2 * group * seq_len * width * hidden_cols,
        in_specs=[whole(v.shape) for v in out_ins]
        + [pl.BlockSpec((w.shape[0], TILE), lambda *_: (0, 2)) for ws in w_mlp for w in ws],
    )
    out_sum = collect(*out_terms, [], [attn_grad[0]])
    ins = [tie(attn_grad[0], *parts), attn_grad[1], qkv] + facts + w_attn
    outs = [lin_shape, lin_shape, shaped((group, 1, 3 * head_cols), F32), mine3, other3]
    lin_own, lin_sib, bias_sums, *terms = call(
        functools.partial(attend_back_kernel, len(w_attn)),
        ins,
        outs,
        attn_flops,
        in_specs=[each(v.shape) for v in ins[: 3 + len(facts)]] + [whole(v.shape) for v in w_attn],
        out_specs=[each(v.shape) for v in outs],
        grid=(group,),
        scratch=[lines, pltpu.VMEM((seq_len, 3 * head_cols), BF)],
    )
    bias_sums = jnp.sum(bias_sums, axis=(0, 1))
    in_grad = collect(*map(half, terms), [], [out_sum])
    attn_steps = weight_grads(
        [
            (seq_in, [[half(lin_own), half(lin_sib)]]),
            ([half(h) for h in attn_grad], [mixed]),
        ],
        1,
    )
    parts, _ = attn_steps.send(None)
    more, _ = attn_steps.send(parts + [p for c in came_two for p in c])
    token_grad = from_rel(resid_grad + norm_back(in_grad, normed_one, inv_one, gains[0]))

    def sum_all(array):
        for b in far_bits + list(GROUP_BITS):
            array = array + swap(array, 1 << b)
            yield array
        yield array + sibling(array)

    def both_sums(grad, normed):
        return [jnp.sum(grad * normed, axis=0), jnp.sum(grad, axis=0)]

    norm_sums = jnp.stack(both_sums(in_grad, normed_one) + both_sums(mid_local, normed_two))
    bias_full = lax.dynamic_update_slice(
        jnp.zeros((3, head_cols * group * lax.axis_size("tensor")), F32),
        bias_sums.reshape(3, head_cols),
        (jnp.int32(0), (core * group + rank) * head_cols),
    )
    sums = list(sum_all(jnp.concatenate([from_rel(norm_sums), bias_full])))
    result = from_rel((resid_two + out_sum).astype(BF))
    after = [in_grad]
    mlp_came = []
    for t, steps in enumerate(mlp_steps):
        *_, (mlp_mine, _) = [steps.send(more)] + list(steps)
        mlp_came.append(exchange(tie(mlp_mine[0], *after)))
        after = [mlp_came[-1], sums[t]]
    *_, (attn_mine, _) = list(attn_steps)
    attn_came = exchange(tie(attn_mine[0], *after))
    gate_up_grad, down_grad = finish(
        finish_mlp_kernel, mlp_came, (gate_up_weight.shape, down_weight.shape)
    )
    qkv_grad, out_w_grad = finish(
        finish_attn_kernel, [attn_came], (qkv_weight.shape, out_weight.shape)
    )
    sums = sums[-1]
    return (
        result,
        token_grad,
        sums[0],
        sums[1],
        qkv_grad,
        sums[4:],
        out_w_grad,
        sums[2],
        sums[3],
        gate_up_grad,
        down_grad,
    )


def solution(mesh):
    return jax.shard_map(
        on_device,
        mesh=mesh,
        in_specs=(
            P(("dp", "tensor"), None),
            P("dp"),
            P(),
            P(),
            P(None, "dp", "tensor"),
            P(None, "tensor"),
            P("tensor", "dp"),
            P(),
            P(),
            P(None, "dp", "tensor"),
            P("tensor", "dp"),
            P(("dp", "tensor"), None),
        ),
        out_specs=(
            P(("dp", "tensor"), None),
            P(("dp", "tensor"), None),
            P(),
            P(),
            P(None, "dp", "tensor"),
            P(),
            P("tensor", "dp"),
            P(),
            P(),
            P(None, "dp", "tensor"),
            P("tensor", "dp"),
        ),
        check_vma=False,
    )
```

```python
import functools

import jax
import jax.numpy as jnp
from jax import lax
from jax.experimental import pallas as pl
from jax.experimental.pallas import tpu as pltpu
from jax.sharding import PartitionSpec as P

HD = 64
ROT = 16
LANES = 128

norm_eps = 1e-05
rope_base = 10000.0
score_scale = 0.125
masked_score = -1e30

GROUP_BITS = (1, 2)
BF = jnp.bfloat16
F32 = jnp.float32
VMEM_LIMIT = 60 * 1024 * 1024


def doc_positions(segment):
    token_index = jnp.arange(segment.shape[0], dtype=jnp.int32)
    begins = jnp.concatenate([jnp.ones((1,), dtype=jnp.bool_), segment[1:] != segment[:-1]])
    starts = lax.cummax(jnp.where(begins, token_index, jnp.zeros_like(token_index)), axis=0)
    return token_index - starts


def norm_parts(values, gain, shift):
    row_mean = jnp.mean(values, axis=-1, keepdims=True)
    centred = values - row_mean
    inv_std = lax.rsqrt(jnp.mean(centred * centred, axis=-1, keepdims=True) + norm_eps)
    normed = centred * inv_std
    return (normed * gain + shift, normed, inv_std)


def norm_back(incoming, normed, inv_std, gain):
    scaled = incoming * gain
    adjusted = (
        scaled
        - jnp.mean(scaled, axis=-1, keepdims=True)
        - normed * jnp.mean(scaled * normed, axis=-1, keepdims=True)
    )
    return adjusted * inv_std


def dot(a, b, a_dim, b_dim):
    return lax.dot_general(
        a, b, (((a_dim,), (b_dim,)), ((), ())), preferred_element_type=F32
    )


def whole(shape, once=False):
    zeros = (0,) * len(shape)
    return pl.BlockSpec(
        shape, lambda *_: zeros, pipeline_mode=pl.Buffered(buffer_count=1) if once else None
    )


def each(shape):
    zeros = (0,) * (len(shape) - 1)
    return pl.BlockSpec((None,) + shape[1:], lambda k, *_: (k,) + zeros)


LONG, SHORT = 30, 0


def call(
    kernel, ins, out_shapes, flops, in_specs=None, out_specs=None, grid=(1,), scratch=(), cost=LONG
):
    moved = cost * sum(v.size * v.dtype.itemsize for v in [*ins, *out_shapes])
    return pl.pallas_call(
        kernel,
        grid=grid,
        in_specs=in_specs or [whole(v.shape) for v in ins],
        out_specs=out_specs or [whole(s.shape) for s in out_shapes],
        out_shape=list(out_shapes),
        scratch_shapes=list(scratch),
        compiler_params=pltpu.CompilerParams(vmem_limit_bytes=VMEM_LIMIT),
        cost_estimate=pl.CostEstimate(flops=cost * flops, bytes_accessed=moved, transcendentals=0),
    )(*ins)


def shaped(shape, dtype):
    return jax.ShapeDtypeStruct(shape, dtype)


def deal(cols, group):
    full = cols // (LANES * group) * LANES
    share = (cols - full * group) // group
    return full, share


def pack_attn_kernel(group, qkv_ref, out_ref, sent_ref):
    cols = qkv_ref.shape[2] // group
    block = qkv_ref.shape[1]
    for k in range(group):
        at, here = slice(k * cols, (k + 1) * cols), slice(k * block, (k + 1) * block)
        for j in range(3):
            sent_ref[here, j * cols : (j + 1) * cols] = qkv_ref[j, :, at]
        sent_ref[here, 3 * cols :] = out_ref[at, :].T


TILE = 2 * LANES


def column(j, at):
    return at // TILE * 3 * TILE + j * TILE + at % TILE


def pack_mlp_kernel(group, gate_up_ref, down_ref, sent_ref):
    full, share = deal(gate_up_ref.shape[2], group)
    block = gate_up_ref.shape[1]
    per = LANES // share
    lane = lax.broadcasted_iota(jnp.int32, (1, LANES), 1) // share
    for k in range(group):
        here = slice(k * block, (k + 1) * block)
        for at in range(0, full + LANES, LANES):
            own = at < full
            start = k * full + at if own else group * full + k // per * LANES
            take = slice(start, start + LANES)
            for j in range(3):
                value = gate_up_ref[j, :, take] if j < 2 else down_ref[take, :].T
                if not own:
                    value = jnp.where(lane == k % per, value, 0).astype(BF)
                to = column(j, at)
                sent_ref[here, to : to + LANES] = value


def finish_mlp_kernel(group, *refs):
    got, gate_up_ref, down_ref = refs
    full, share = deal(gate_up_ref.shape[2], group)
    block = gate_up_ref.shape[1]
    per = LANES // share

    def taken(k, j, at):
        to = column(j, at)
        return got[k * block : (k + 1) * block, to : to + LANES].astype(F32)

    for j in range(3):
        for at in range(0, full + LANES, LANES):
            own = at < full
            for k in range(0, group, 1 if own else per):
                start = k * full + at if own else group * full + k // per * LANES
                take = slice(start, start + LANES)
                value = sum(taken(k + i, j, at) for i in range(1 if own else per))
                if j < 2:
                    gate_up_ref[j, :, take] = value
                else:
                    down_ref[take, :] = value.T


def finish_attn_kernel(group, got_ref, qkv_ref, out_ref):
    cols = qkv_ref.shape[2] // group
    block = qkv_ref.shape[1]
    for k in range(group):
        here, at = slice(k * block, (k + 1) * block), slice(k * cols, (k + 1) * cols)
        for j in range(3):
            qkv_ref[j, :, at] = got_ref[here, j * cols : (j + 1) * cols].astype(F32)
        out_ref[at, :] = got_ref[here, 3 * cols :].astype(F32).T


def spans(weights):
    at = 0
    for w in weights:
        yield slice(at, at + w.shape[0]), w
        at += w.shape[0]


def turn(value, tables, sign):
    cosine, lead, tail = tables
    ahead = pltpu.roll(value, LANES - ROT // 2, 1)
    behind = pltpu.roll(value, ROT // 2, 1)
    return value * cosine + (ahead * lead + behind * tail) * sign


def soft(queries, keys, mask):
    scores = dot(queries, keys, 1, 1) * score_scale + mask
    weights = jnp.exp(scores - jnp.max(scores, axis=-1, keepdims=True))
    return weights * (1.0 / jnp.sum(weights, axis=-1, keepdims=True))


def own_head(half):
    return lax.broadcasted_iota(jnp.int32, (1, LANES), 1) // HD == half


def attend_kernel(far, own_ref, sib_ref, bias_ref, mask_ref, cos_ref, lead_ref, tail_ref, *refs):
    weights, refs = refs[:far], refs[far:]
    qkv_ref, mixed_own, mixed_sib, mine_ref, other_ref, lines, mixed_ref = refs
    rows = mine_ref.shape[0]
    lines[:rows] = own_ref[...]
    lines[rows:] = sib_ref[...]
    cols = mixed_ref.shape[1]
    tables = (cos_ref[...], lead_ref[...], tail_ref[...])
    lin = bias_ref[...]
    for at, w in spans(weights):
        lin = lin + dot(lines[:, at], w[:, : 3 * cols], 1, 0)
    mask = mask_ref[...]
    for i in range(cols // LANES):
        at = [slice(j * cols + i * LANES, j * cols + (i + 1) * LANES) for j in range(3)]
        queries = turn(lin[:, at[0]], tables, 1.0).astype(BF)
        keys = turn(lin[:, at[1]], tables, 1.0).astype(BF)
        values = lin[:, at[2]].astype(BF)
        qkv_ref[:, at[0]] = queries
        qkv_ref[:, at[1]] = keys
        qkv_ref[:, at[2]] = values
        mixed = None
        for half in range(LANES // HD):
            here = own_head(half)
            probs = soft(jnp.where(here, queries, 0).astype(BF), keys, mask).astype(BF)
            part = dot(probs, values, 1, 0)
            mixed = part if mixed is None else jnp.where(here, part, mixed)
        mixed_ref[:, i * LANES : (i + 1) * LANES] = mixed.astype(BF)
    mixed_own[...] = mixed_ref[:rows]
    mixed_sib[...] = mixed_ref[rows:]
    for at, w in spans(weights):
        term = dot(mixed_ref[...], w[:, 3 * cols :], 1, 1)
        mine_ref[:, at] = term[:rows]
        other_ref[:, at] = term[rows:].astype(BF)


def attend_back_kernel(far, own_ref, sib_ref, qkv_ref, mask_ref, cos_ref, lead_ref, tail_ref, *refs):
    weights, refs = refs[:far], refs[far:]
    lin_own, lin_sib, sums_ref, mine_ref, other_ref, lines, lin_ref = refs
    rows = own_ref.shape[0]
    lines[:rows] = own_ref[...]
    lines[rows:] = sib_ref[...]
    cols = qkv_ref.shape[1] // 3
    tables = (cos_ref[...], lead_ref[...], tail_ref[...])
    mixed_grad = sum(dot(lines[:, at], w[:, 3 * cols :], 1, 0) for at, w in spans(weights))
    mixed_grad = mixed_grad.astype(BF)
    mask = mask_ref[...]
    for i in range(cols // LANES):
        at = [slice(j * cols + i * LANES, j * cols + (i + 1) * LANES) for j in range(3)]
        queries, keys, values = (qkv_ref[:, a] for a in at)
        grad = mixed_grad[:, i * LANES : (i + 1) * LANES]
        found = [None] * 3
        for half in range(LANES // HD):
            here = own_head(half)
            probs = soft(jnp.where(here, queries, 0).astype(BF), keys, mask)
            value_grad = dot(probs.astype(BF), grad, 0, 0)
            prob_grad = dot(jnp.where(here, grad, 0).astype(BF), values, 1, 1)
            score_grad = (
                probs * (prob_grad - jnp.sum(probs * prob_grad, axis=-1, keepdims=True))
            ).astype(BF)
            query_grad = dot(score_grad, keys, 1, 0)
            key_grad = dot(score_grad, queries, 0, 0)
            parts = (query_grad, key_grad, value_grad)
            found = [p if f is None else jnp.where(here, p, f) for p, f in zip(parts, found)]
        lin_ref[:, at[0]] = turn(found[0] * score_scale, tables, -1.0).astype(BF)
        lin_ref[:, at[1]] = turn(found[1] * score_scale, tables, -1.0).astype(BF)
        lin_ref[:, at[2]] = found[2].astype(BF)
    lin_own[...] = lin_ref[:rows]
    lin_sib[...] = lin_ref[rows:]
    sums_ref[...] = jnp.sum(lin_ref[...].astype(F32), axis=0, keepdims=True)
    for at, w in spans(weights):
        term = dot(lin_ref[...], w[:, : 3 * cols], 1, 1)
        mine_ref[:, at] = term[:rows]
        other_ref[:, at] = term[rows:].astype(BF)


def mlp_kernel(far, tiles, first, *refs):
    lines, grads, refs = refs[:2], refs[2:4], refs[4:]
    before, refs = (None, refs) if first else (refs[:2], refs[2:])
    weights, refs = refs[: far * tiles], refs[far * tiles :]
    found, sums, (held, held_grad) = refs[: 4 * tiles], refs[-4:-2], refs[-2:]
    rows = lines[0].shape[0]
    for half in range(2):
        here = slice(half * rows, (half + 1) * rows)
        held[here] = lines[half][...]
        held_grad[here] = grads[half][...]
    inner = []
    for t in range(tiles):
        mine = weights[t * far : (t + 1) * far]
        gate_up = sum(dot(held[:, at], w[:, : 2 * TILE], 1, 0) for at, w in spans(mine))
        hidden_grad = sum(dot(held_grad[:, at], w[:, 2 * TILE :], 1, 0) for at, w in spans(mine))
        gate_pre, up_values = gate_up[:, :TILE], gate_up[:, TILE:]
        gate_sig = jax.nn.sigmoid(gate_pre)
        smooth = gate_pre * gate_sig
        gate_grad = hidden_grad * up_values * gate_sig * (1.0 + gate_pre * (1.0 - gate_sig))
        hidden = (smooth * up_values).astype(BF)
        pair = jnp.concatenate([gate_grad.astype(BF), (hidden_grad * smooth).astype(BF)], axis=1)
        for half in range(2):
            here = slice(half * rows, (half + 1) * rows)
            found[4 * t + half][...] = pair[here]
            found[4 * t + 2 + half][...] = hidden[here]
        inner.append(pair)
    for p, (at, _) in enumerate(spans(weights[:far])):
        term = sum(
            dot(pair, weights[t * far + p][:, : 2 * TILE], 1, 1) for t, pair in enumerate(inner)
        )
        for half in range(2):
            part = term[half * rows : (half + 1) * rows]
            if not first:
                part = part + before[half][:, at]
            sums[half][:, at] = part.astype(sums[half].dtype)


def mlp_out_kernel(far, tiles, *refs):
    hiddens, refs = refs[: 2 * tiles], refs[2 * tiles :]
    weights, outs = refs[: far * tiles], refs[far * tiles :]
    for half in range(2):
        for p, (at, _) in enumerate(spans(weights[:far])):
            term = sum(
                dot(hiddens[2 * t + half][...], weights[t * far + p][...], 1, 1)
                for t in range(tiles)
            )
            outs[half][:, at] = term.astype(outs[half].dtype)


def grad_kernel(kinds, adds, *refs):
    lefts, rights = [], []
    at = 0
    for count in kinds:
        lefts.append(refs[at : at + 2])
        rights.append([refs[at + 2 + 2 * c : at + 4 + 2 * c] for c in range(count)])
        at += 2 + 2 * count
    more, out = refs[at : at + len(adds)], refs[-1]
    start = 0
    for left, columns in zip(lefts, rights):
        for right in columns:
            here = slice(start, start + right[0].shape[1])
            start = here.stop
            total = sum(dot(a[...], b[...], 0, 0) for a, b in zip(left, right))
            for extra, first in zip(more, adds):
                if first <= here.start < first + extra.shape[1]:
                    total = total + extra[:, here.start - first : here.stop - first].astype(F32)
            out[:, here] = total.astype(BF)


def copies_kernel(local_ref, out_ref):
    for k in range(out_ref.shape[0]):
        out_ref[k] = local_ref[...]


def on_device(
    tokens,
    segment_ids,
    ln1_gain,
    ln1_bias,
    qkv_weight,
    qkv_bias,
    out_weight,
    ln2_gain,
    ln2_bias,
    gate_up_weight,
    down_weight,
    out_grad,
):
    dp_size = lax.axis_size("dp")
    bits = dp_size.bit_length() - 1
    me = lax.axis_index("dp")
    core = lax.axis_index("tensor")
    rows, width = tokens.shape
    seq_len = segment_ids.shape[0]
    group = 1 << len(GROUP_BITS)
    far_bits = [b for b in reversed(range(bits)) if b not in GROUP_BITS]
    masks = [
        sum(1 << b for i, b in enumerate(GROUP_BITS) if (k >> i) & 1) for k in range(group)
    ]
    my_bit = [(me >> b) & 1 for b in range(bits)]
    rank = sum(my_bit[b] << i for i, b in enumerate(GROUP_BITS))
    heads = qkv_bias.shape[1] // HD // group
    head_cols = heads * HD
    hidden_cols = deal(down_weight.shape[0], group)[0] + LANES

    def swap(array, mask):
        if mask == 0:
            return array
        return lax.ppermute(array, "dp", [(d, d ^ mask) for d in range(dp_size)])

    def sibling(array):
        return lax.ppermute(array, "tensor", [(0, 1), (1, 0)])

    order = [bits - 1 - b for b in reversed(far_bits)]
    order += [bits - 1 - b for b in reversed(GROUP_BITS)]

    def swapped(array, axis, bit):
        low, high = jnp.split(array, 2, axis)
        low, high = jnp.where(bit == 1, high, low), jnp.where(bit == 1, low, high)
        return jnp.concatenate([low, high], axis)

    def to_rel(array):
        lead = array.ndim - 1
        cut = array.reshape(array.shape[:-1] + (2,) * bits + (width // dp_size,))
        cut = cut.transpose(list(range(lead)) + [lead + o for o in order] + [lead + bits])
        for i, b in enumerate(reversed(far_bits)):
            cut = swapped(cut, lead + i, my_bit[b])
        return cut.reshape(array.shape)

    def from_rel(array):
        lead = array.ndim - 1
        cut = array.reshape(array.shape[:-1] + (2,) * bits + (width // dp_size,))
        for i, b in enumerate(reversed(far_bits)):
            cut = swapped(cut, lead + i, my_bit[b])
        back = [order.index(i) for i in range(bits)]
        cut = cut.transpose(list(range(lead)) + [lead + o for o in back] + [lead + bits])
        return cut.reshape(array.shape)

    block = width // dp_size
    shard_rows = group * block
    far = 1 << len(far_bits)
    bands = [
        [d for d in range(dp_size) if all((d ^ first) >> b & 1 == 0 for b in far_bits)]
        for first in range(dp_size)
        if all(first >> b & 1 == 0 for b in GROUP_BITS)
    ]

    def exchange(rows_by_rank):
        return lax.all_to_all(rows_by_rank, "dp", 0, 0, axis_index_groups=bands, tiled=True)

    def tie(value, *after):
        return lax.optimization_barrier((value, *after))[0]

    def pack(kernel, ins, cols):
        return call(
            functools.partial(kernel, group), ins, [shaped((shard_rows, cols), BF)], 0
        )[0]

    def gather(shard, after=(), after_own=()):
        pieces = [shard]
        for n, b in enumerate(far_bits):
            own = tie(shard, *(after_own if n else after))
            pieces = pieces + [swap(p, 1 << b) for p in [own] + pieces[1:]]
        return pieces

    def copies(local):
        return jnp.broadcast_to(local, (group,) + local.shape)

    def spread(copied, after=(), then=()):
        mine = exchange(tie(copied, *after))
        return mine, sibling(tie(mine, *then))

    def half(array):
        return array.reshape((-1,) + array.shape[2:])

    def by_block(array):
        return array.reshape((group, -1) + array.shape[1:])

    def merge(mine, other, after=()):
        other = sibling(tie(other, *after))
        return (by_block(mine) + by_block(other).astype(F32)).astype(BF)

    def collect(both, after=()):
        return jnp.sum(exchange(tie(both, *after)).astype(F32), axis=0)

    wide = sorted(range(1, far), key=lambda i: (-i.bit_length(), -i))

    def below(i):
        bits_left = range(i.bit_length(), len(far_bits))
        return [c for b in bits_left for c in below(i | 1 << b) + [i | 1 << b]]

    def block_grad(i, kinds, adds, after=()):
        cols = sum(c[0].shape[1] for _, sets in kinds for c in sets)
        ins, specs = [], []
        for left, sets in kinds:
            ins += left
            specs += [pl.BlockSpec((v.shape[0], shard_rows), lambda *_: (0, i)) for v in left]
            for s in sets:
                ins += s
                specs += [whole(v.shape) for v in s]
        ins += [v for v, _ in adds]
        specs += [whole(v.shape) for v, _ in adds]
        ins[0] = tie(ins[0], *after)
        return call(
            functools.partial(grad_kernel, [len(s) for _, s in kinds], [at for _, at in adds]),
            ins,
            [shaped((shard_rows, cols), BF)],
            2 * group * seq_len * shard_rows * cols,
            in_specs=specs,
        )[0]

    def send(i, part):
        return swap(part, 1 << far_bits[i.bit_length() - 1])

    def parent(i):
        return i ^ 1 << i.bit_length() - 1

    def finish(kernel, came, shapes):
        return call(functools.partial(kernel, group), came, [shaped(s, F32) for s in shapes], 0)

    gains = to_rel(jnp.stack([ln1_gain, ln1_bias, ln2_gain, ln2_bias]))
    resid = to_rel(tokens).astype(F32)
    normed_in, normed_one, inv_one = norm_parts(resid, gains[0], gains[1])
    seq_local = normed_in.astype(BF)
    attn_pack = pack(pack_attn_kernel, [qkv_weight, out_weight], 4 * head_cols)
    attn_shard = exchange(attn_pack)
    segs = jnp.stack([swap(tie(segment_ids, attn_pack), m) for m in masks])
    segs = segs.reshape((2,) * len(GROUP_BITS) + segs.shape[1:])
    for i, b in enumerate(reversed(GROUP_BITS)):
        segs = swapped(segs, i, my_bit[b])
    segs = segs.reshape(group, seq_len)
    mlp_pack = pack(pack_mlp_kernel, [tie(gate_up_weight, attn_shard), down_weight], 3 * hidden_cols)
    mlp_shard = exchange(tie(mlp_pack, attn_shard))
    w_attn = gather(attn_shard)
    tiles = hidden_cols // TILE
    spots = jax.vmap(doc_positions)(segs)
    segs, spots = (jnp.where(core == 1, jnp.roll(v, rows, axis=1), v) for v in (segs, spots))
    index = jnp.arange(seq_len, dtype=jnp.int32)
    index = jnp.where(core == 1, jnp.roll(index, rows), index)
    allowed = (segs[:, :, None] == segs[:, None, :]) & (index[None, :] <= index[:, None])
    mask = jnp.where(allowed, 0.0, masked_score).astype(F32)
    dim = jnp.arange(LANES, dtype=jnp.int32) % HD
    pair = (dim % (ROT // 2)).astype(F32)
    speed = jnp.where(dim < ROT, rope_base ** (-2.0 * pair / ROT), 0.0)
    angles = spots.astype(F32)[..., None] * speed
    cosine, sine = jnp.cos(angles), jnp.sin(angles)
    lead = jnp.where(dim < ROT // 2, -sine, 0.0)
    tail = jnp.where((dim >= ROT // 2) & (dim < ROT), sine, 0.0)

    w_mlp = []
    after, after_own = [w_attn[1]], [w_attn[-1]]
    for t in range(tiles):
        shard = mlp_shard[:, t * 3 * TILE : (t + 1) * 3 * TILE]
        w_mlp.append(gather(shard, after, after_own))
        after, after_own = [w_mlp[t][1]], [w_mlp[t][2]]
    grad_local = to_rel(out_grad)
    grad_copies = copies(grad_local)
    heard = spread(
        tie(copies(seq_local), grad_copies, cosine, lead, tail, mask),
        [mlp_shard] + w_attn[1:3],
        w_attn[3:] + w_mlp[0][1:2],
    )
    seq_in = [half(h) for h in heard]
    grad_rows = spread(grad_copies, [heard[0]])

    bias = lax.dynamic_slice_in_dim(qkv_bias, rank * head_cols, head_cols, 1).reshape(1, -1)
    facts = [mask, cosine, lead, tail]
    lines = pltpu.VMEM((seq_len, width), BF)
    mine, other = shaped((group * rows, width), F32), shaped((group * rows, width), BF)
    mine3, other3 = (shaped((group, rows, width), t) for t in (F32, BF))
    qkv_shape = shaped((group, seq_len, 3 * head_cols), BF)
    mixed_shape = shaped((group, rows, head_cols), BF)
    lin_shape = shaped((group, rows, 3 * head_cols), BF)
    attn_flops = 2 * group * seq_len * width * 4 * head_cols

    ins = [*heard, bias] + facts + w_attn
    outs = [qkv_shape, mixed_shape, mixed_shape, mine3, other3]
    qkv, mixed_own, mixed_sib, *terms = call(
        functools.partial(attend_kernel, len(w_attn)),
        ins,
        outs,
        attn_flops,
        in_specs=[each(v.shape) for v in heard]
        + [whole(bias.shape)]
        + [each(v.shape) for v in facts]
        + [whole(v.shape) for v in w_attn],
        out_specs=[each(v.shape) for v in outs],
        grid=(group,),
        scratch=[lines, pltpu.VMEM((seq_len, head_cols), BF)],
    )
    mixed = [half(mixed_own), half(mixed_sib)]
    both = merge(*map(half, terms), w_mlp[0][2:3])
    attn_sum = collect(both, [grad_rows[0]])
    resid_two = resid + tie(attn_sum, *w_mlp[0][3:], *w_mlp[1][1:3])
    normed_mid, normed_two, inv_two = norm_parts(resid_two, gains[2], gains[3])
    seq_mid = [half(h) for h in spread(copies(normed_mid.astype(BF)), (), w_mlp[1][3:] + [p for w in w_mlp[2:] for p in w[1:3]])]
    grad_rows = [half(h) for h in grad_rows]

    row_spec = pl.BlockSpec((rows, width), lambda k: (k, 0))
    pair_spec, hidden_spec = (pl.BlockSpec((rows, n * TILE), lambda k: (k, 0)) for n in (2, 1))
    pair_shape, hidden_shape = (shaped((group * rows, n * TILE), BF) for n in (2, 1))
    weights = [[w for w in [mlp_shard] + w_mlp[t][1:]] for t in range(tiles)]
    inner, mid = [], []
    for batch in (range(tiles - 1), range(tiles - 1, tiles)):
        ins = [*seq_mid, *grad_rows] + mid
        final = batch[-1] == tiles - 1
        *found, mid_own, mid_sib = call(
            functools.partial(mlp_kernel, far, len(batch), not mid),
            ins + [w for t in batch for w in weights[t]],
            ([pair_shape] * 2 + [hidden_shape] * 2) * len(batch) + [mine, other if final else mine],
            10 * group * seq_len * width * TILE * len(batch),
            in_specs=[row_spec] * len(ins)
            + [
                pl.BlockSpec((w.shape[0], 3 * TILE), lambda *_, t=0 if n else t: (0, t))
                for t in batch
                for n, w in enumerate(weights[t])
            ],
            out_specs=([pair_spec] * 2 + [hidden_spec] * 2) * len(batch) + [row_spec] * 2,
            grid=(group,),
            scratch=[lines, lines],
        )
        inner += found
        mid = [mid_own, mid_sib]
    weights = [w for ws in weights for w in ws]
    hiddens = [inner[4 * t + 2 : 4 * t + 4] for t in range(tiles)]
    tile_kinds = [
        [(seq_mid, [inner[4 * t : 4 * t + 2]]), (grad_rows, [hiddens[t]])] for t in range(tiles)
    ]
    all_kinds = [kind for kinds in tile_kinds for kind in kinds]
    both = merge(mid_own, mid_sib)

    last = far // 2
    batches = [range(t, t + 1) for t in range(tiles)]
    batch_kinds = [[kind for t in batch for kind in tile_kinds[t]] for batch in batches]
    batch_adds = [[[] for _ in range(far)] for _ in batches]
    first_parts, first_came, later, later_came, held = [], [], [], [], []

    def batch_step(n, i, after):
        part = block_grad(i, batch_kinds[n], [(v, 0) for v in batch_adds[n][i]], after)
        if i == 1 and n > 1:
            held.append((n, i, part))
            return part, None
        came = send(i, part)
        batch_adds[n][parent(i)].append(came)
        return part, came

    steps = [i for i in below(0) if i != last]
    for n in range(len(batches)):
        part, came = batch_step(n, steps[0], [both] + first_parts if n else [])
        first_parts.append(part)
        first_came.append(came)
    last_part = block_grad(last, all_kinds, [], first_parts)
    last_came = send(last, last_part)
    mid_local = tie(collect(both), last_part, first_came[0])
    resid_grad = grad_local.astype(F32) + norm_back(mid_local, normed_two, inv_two, gains[2])
    resid_back = resid_grad.astype(BF)
    copied = copies(resid_back)
    for i in steps[1:]:
        for n in range(len(batches)):
            part, came = batch_step(n, i, [copied] + later)
            later.append(part)
            later_came.append(came)
    out_ins = [h for pair in hiddens for h in pair]
    out_ins[0] = tie(out_ins[0], copied)
    out_terms = call(
        functools.partial(mlp_out_kernel, far, tiles),
        out_ins + weights,
        [mine, other],
        2 * group * seq_len * width * hidden_cols,
        in_specs=[whole(v.shape) for v in out_ins]
        + [
            pl.BlockSpec((w.shape[0], TILE), lambda *_, t=3 * (n // far) if n % far == 0 else 0: (0, t + 2))
            for n, w in enumerate(weights)
        ],
        cost=SHORT,
    )
    out_both = merge(*out_terms)
    attn_grad = spread(copied, [], [out_both, *later, later_came[0], last_came])
    ins = [*attn_grad, qkv] + facts + w_attn
    outs = [lin_shape, lin_shape, shaped((group, 1, 3 * head_cols), F32), mine3, other3]
    lin_own, lin_sib, bias_sums, *terms = call(
        functools.partial(attend_back_kernel, len(w_attn)),
        ins,
        outs,
        attn_flops,
        in_specs=[each(v.shape) for v in ins[: 3 + len(facts)]] + [whole(v.shape) for v in w_attn],
        out_specs=[each(v.shape) for v in outs],
        grid=(group,),
        scratch=[lines, pltpu.VMEM((seq_len, 3 * head_cols), BF)],
    )
    bias_sums = jnp.sum(bias_sums, axis=(0, 1))
    for n, i, part in held:
        came = send(i, tie(part, lin_own))
        batch_adds[n][parent(i)].append(came)
        later_came.append(came)
    later_came = [came for came in later_came if came is not None]
    both = merge(*map(half, terms), later_came[1:2])
    out_sum = collect(out_both, [attn_grad[0]])
    in_grad = tie(collect(both, [out_sum]), *later_came[2:3])
    attn_kinds = [
        (seq_in, [[half(lin_own), half(lin_sib)]]),
        ([half(h) for h in attn_grad], [mixed]),
    ]
    attn_adds = [[] for _ in range(far)]
    parts, attn_sent = [], []
    for n, i in enumerate(wide):
        after = ([in_grad] if attn_adds[i] else [both]) + parts if n else []
        part = block_grad(i, attn_kinds, [(v, 0) for v in attn_adds[i]], after)
        parts.append(part)
        attn_sent.append(send(i, part))
        attn_adds[parent(i)].append(attn_sent[-1])
    token_grad = from_rel(resid_grad + norm_back(in_grad, normed_one, inv_one, gains[0]))

    def sum_all(array):
        array = array + sibling(array)
        yield sum((swap(array, m) for m in masks[1:]), array)

    def far_sum(array):
        for at in range(0, len(far_bits), 2):
            pair = [1 << b for b in far_bits[at : at + 2]]
            array = sum((swap(array, m) for m in pair + [sum(pair)][: len(pair) - 1]), array)
        return array

    def both_sums(grad, normed):
        return [jnp.sum(grad * normed, axis=0), jnp.sum(grad, axis=0)]

    norm_sums = jnp.stack(both_sums(in_grad, normed_one) + both_sums(mid_local, normed_two))
    bias_full = lax.dynamic_update_slice(
        jnp.zeros((3, head_cols * group * lax.axis_size("tensor")), F32),
        bias_sums.reshape(3, head_cols),
        (jnp.int32(0), (core * group + rank) * head_cols),
    )
    sums = list(sum_all(jnp.concatenate([from_rel(norm_sums), bias_full])))
    sums.append(far_sum(sums[0]))
    result = from_rel((resid_two + out_sum).astype(BF))
    adds = [(v, 3 * TILE * b[0]) for b, into in zip(batches, batch_adds) for v in into[0]]
    adds.append((last_came, 0))
    mlp_came = exchange(tie(block_grad(0, all_kinds, adds, parts), in_grad))
    attn_mine = block_grad(0, attn_kinds, [(v, 0) for v in attn_adds[0]], sums[1:])
    attn_came = exchange(tie(attn_mine, mlp_came))
    gate_up_grad, down_grad = finish(
        finish_mlp_kernel, [mlp_came], (gate_up_weight.shape, down_weight.shape)
    )
    qkv_grad, out_w_grad = finish(
        finish_attn_kernel, [attn_came], (qkv_weight.shape, out_weight.shape)
    )
    sums = sums[-1]
    return (
        result,
        token_grad,
        sums[0],
        sums[1],
        qkv_grad,
        sums[4:],
        out_w_grad,
        sums[2],
        sums[3],
        gate_up_grad,
        down_grad,
    )


def solution(mesh):
    return jax.shard_map(
        on_device,
        mesh=mesh,
        in_specs=(
            P(("dp", "tensor"), None),
            P("dp"),
            P(),
            P(),
            P(None, "dp", "tensor"),
            P(None, "tensor"),
            P("tensor", "dp"),
            P(),
            P(),
            P(None, "dp", "tensor"),
            P("tensor", "dp"),
            P(("dp", "tensor"), None),
        ),
        out_specs=(
            P(("dp", "tensor"), None),
            P(("dp", "tensor"), None),
            P(),
            P(),
            P(None, "dp", "tensor"),
            P(),
            P("tensor", "dp"),
            P(),
            P(),
            P(None, "dp", "tensor"),
            P("tensor", "dp"),
        ),
        check_vma=False,
    )
```

```python
import functools

import jax
import jax.numpy as jnp
from jax import lax
from jax.experimental import pallas as pl
from jax.experimental.pallas import tpu as pltpu
from jax.sharding import PartitionSpec as P

HD = 64
ROT = 16
LANES = 128

norm_eps = 1e-05
rope_base = 10000.0
score_scale = 0.125
masked_score = -1e30

GROUP_BITS = (1, 2)
BF = jnp.bfloat16
F32 = jnp.float32
VMEM_LIMIT = 60 * 1024 * 1024


def doc_positions(segment):
    token_index = jnp.arange(segment.shape[0], dtype=jnp.int32)
    begins = jnp.concatenate([jnp.ones((1,), dtype=jnp.bool_), segment[1:] != segment[:-1]])
    starts = lax.cummax(jnp.where(begins, token_index, jnp.zeros_like(token_index)), axis=0)
    return token_index - starts


def norm_parts(values, gain, shift):
    row_mean = jnp.mean(values, axis=-1, keepdims=True)
    centred = values - row_mean
    inv_std = lax.rsqrt(jnp.mean(centred * centred, axis=-1, keepdims=True) + norm_eps)
    normed = centred * inv_std
    return (normed * gain + shift, normed, inv_std)


def norm_back(incoming, normed, inv_std, gain):
    scaled = incoming * gain
    adjusted = (
        scaled
        - jnp.mean(scaled, axis=-1, keepdims=True)
        - normed * jnp.mean(scaled * normed, axis=-1, keepdims=True)
    )
    return adjusted * inv_std


def dot(a, b, a_dim, b_dim):
    return lax.dot_general(
        a, b, (((a_dim,), (b_dim,)), ((), ())), preferred_element_type=F32
    )


def whole(shape, once=False):
    zeros = (0,) * len(shape)
    return pl.BlockSpec(
        shape, lambda *_: zeros, pipeline_mode=pl.Buffered(buffer_count=1) if once else None
    )


def each(shape):
    zeros = (0,) * (len(shape) - 1)
    return pl.BlockSpec((None,) + shape[1:], lambda k, *_: (k,) + zeros)


LONG, SHORT = 30, 0


def call(
    kernel, ins, out_shapes, flops, in_specs=None, out_specs=None, grid=(1,), scratch=(), cost=LONG
):
    moved = cost * sum(v.size * v.dtype.itemsize for v in [*ins, *out_shapes])
    return pl.pallas_call(
        kernel,
        grid=grid,
        in_specs=in_specs or [whole(v.shape) for v in ins],
        out_specs=out_specs or [whole(s.shape) for s in out_shapes],
        out_shape=list(out_shapes),
        scratch_shapes=list(scratch),
        compiler_params=pltpu.CompilerParams(vmem_limit_bytes=VMEM_LIMIT),
        cost_estimate=pl.CostEstimate(flops=cost * flops, bytes_accessed=moved, transcendentals=0),
    )(*ins)


def shaped(shape, dtype):
    return jax.ShapeDtypeStruct(shape, dtype)


def deal(cols, group):
    full = cols // (LANES * group) * LANES
    share = (cols - full * group) // group
    return full, share


def pack_attn_kernel(group, qkv_ref, out_ref, sent_ref):
    cols = qkv_ref.shape[2] // group
    block = qkv_ref.shape[1]
    for k in range(group):
        at, here = slice(k * cols, (k + 1) * cols), slice(k * block, (k + 1) * block)
        for j in range(3):
            sent_ref[here, j * cols : (j + 1) * cols] = qkv_ref[j, :, at]
        sent_ref[here, 3 * cols :] = out_ref[at, :].T


TILE = 2 * LANES


def column(j, at):
    return at // TILE * 3 * TILE + j * TILE + at % TILE


def pack_mlp_kernel(group, gate_up_ref, down_ref, sent_ref):
    full, share = deal(gate_up_ref.shape[2], group)
    block = gate_up_ref.shape[1]
    per = LANES // share
    lane = lax.broadcasted_iota(jnp.int32, (1, LANES), 1) // share
    for k in range(group):
        here = slice(k * block, (k + 1) * block)
        for at in range(0, full + LANES, LANES):
            own = at < full
            start = k * full + at if own else group * full + k // per * LANES
            take = slice(start, start + LANES)
            for j in range(3):
                value = gate_up_ref[j, :, take] if j < 2 else down_ref[take, :].T
                if not own:
                    value = jnp.where(lane == k % per, value, 0).astype(BF)
                to = column(j, at)
                sent_ref[here, to : to + LANES] = value


def finish_mlp_kernel(group, *refs):
    got, gate_up_ref, down_ref = refs
    full, share = deal(gate_up_ref.shape[2], group)
    block = gate_up_ref.shape[1]
    per = LANES // share

    def taken(k, j, at):
        to = column(j, at)
        return got[k * block : (k + 1) * block, to : to + LANES].astype(F32)

    for j in range(3):
        for at in range(0, full + LANES, LANES):
            own = at < full
            for k in range(0, group, 1 if own else per):
                start = k * full + at if own else group * full + k // per * LANES
                take = slice(start, start + LANES)
                value = sum(taken(k + i, j, at) for i in range(1 if own else per))
                if j < 2:
                    gate_up_ref[j, :, take] = value
                else:
                    down_ref[take, :] = value.T


def finish_attn_kernel(group, got_ref, qkv_ref, out_ref):
    cols = qkv_ref.shape[2] // group
    block = qkv_ref.shape[1]
    for k in range(group):
        here, at = slice(k * block, (k + 1) * block), slice(k * cols, (k + 1) * cols)
        for j in range(3):
            qkv_ref[j, :, at] = got_ref[here, j * cols : (j + 1) * cols].astype(F32)
        out_ref[at, :] = got_ref[here, 3 * cols :].astype(F32).T


def spans(weights):
    at = 0
    for w in weights:
        yield slice(at, at + w.shape[0]), w
        at += w.shape[0]


def turn(value, tables, sign):
    cosine, lead, tail = tables
    ahead = pltpu.roll(value, LANES - ROT // 2, 1)
    behind = pltpu.roll(value, ROT // 2, 1)
    return value * cosine + (ahead * lead + behind * tail) * sign


def soft(queries, keys, mask):
    scores = dot(queries, keys, 1, 1) * score_scale + mask
    weights = jnp.exp(scores - jnp.max(scores, axis=-1, keepdims=True))
    return weights * (1.0 / jnp.sum(weights, axis=-1, keepdims=True))


def own_head(half):
    return lax.broadcasted_iota(jnp.int32, (1, LANES), 1) // HD == half


def attend_kernel(far, own_ref, sib_ref, bias_ref, mask_ref, cos_ref, lead_ref, tail_ref, *refs):
    weights, refs = refs[:far], refs[far:]
    qkv_ref, mixed_own, mixed_sib, mine_ref, other_ref, lines, mixed_ref = refs
    rows = mine_ref.shape[0]
    lines[:rows] = own_ref[...]
    lines[rows:] = sib_ref[...]
    cols = mixed_ref.shape[1]
    tables = (cos_ref[...], lead_ref[...], tail_ref[...])
    lin = bias_ref[...]
    for at, w in spans(weights):
        lin = lin + dot(lines[:, at], w[:, : 3 * cols], 1, 0)
    mask = mask_ref[...]
    for i in range(cols // LANES):
        at = [slice(j * cols + i * LANES, j * cols + (i + 1) * LANES) for j in range(3)]
        queries = turn(lin[:, at[0]], tables, 1.0).astype(BF)
        keys = turn(lin[:, at[1]], tables, 1.0).astype(BF)
        values = lin[:, at[2]].astype(BF)
        qkv_ref[:, at[0]] = queries
        qkv_ref[:, at[1]] = keys
        qkv_ref[:, at[2]] = values
        mixed = None
        for half in range(LANES // HD):
            here = own_head(half)
            probs = soft(jnp.where(here, queries, 0).astype(BF), keys, mask).astype(BF)
            part = dot(probs, values, 1, 0)
            mixed = part if mixed is None else jnp.where(here, part, mixed)
        mixed_ref[:, i * LANES : (i + 1) * LANES] = mixed.astype(BF)
    mixed_own[...] = mixed_ref[:rows]
    mixed_sib[...] = mixed_ref[rows:]
    for at, w in spans(weights):
        term = dot(mixed_ref[...], w[:, 3 * cols :], 1, 1)
        mine_ref[:, at] = term[:rows].astype(BF)
        other_ref[:, at] = term[rows:].astype(BF)


def attend_back_kernel(far, own_ref, sib_ref, qkv_ref, mask_ref, cos_ref, lead_ref, tail_ref, *refs):
    weights, refs = refs[:far], refs[far:]
    lin_own, lin_sib, sums_ref, mine_ref, other_ref, lines, lin_ref = refs
    rows = own_ref.shape[0]
    lines[:rows] = own_ref[...]
    lines[rows:] = sib_ref[...]
    cols = qkv_ref.shape[1] // 3
    tables = (cos_ref[...], lead_ref[...], tail_ref[...])
    mixed_grad = sum(dot(lines[:, at], w[:, 3 * cols :], 1, 0) for at, w in spans(weights))
    mixed_grad = mixed_grad.astype(BF)
    mask = mask_ref[...]
    for i in range(cols // LANES):
        at = [slice(j * cols + i * LANES, j * cols + (i + 1) * LANES) for j in range(3)]
        queries, keys, values = (qkv_ref[:, a] for a in at)
        grad = mixed_grad[:, i * LANES : (i + 1) * LANES]
        found = [None] * 3
        for half in range(LANES // HD):
            here = own_head(half)
            probs = soft(jnp.where(here, queries, 0).astype(BF), keys, mask)
            value_grad = dot(probs.astype(BF), grad, 0, 0)
            prob_grad = dot(jnp.where(here, grad, 0).astype(BF), values, 1, 1)
            score_grad = (
                probs * (prob_grad - jnp.sum(probs * prob_grad, axis=-1, keepdims=True))
            ).astype(BF)
            query_grad = dot(score_grad, keys, 1, 0)
            key_grad = dot(score_grad, queries, 0, 0)
            parts = (query_grad, key_grad, value_grad)
            found = [p if f is None else jnp.where(here, p, f) for p, f in zip(parts, found)]
        lin_ref[:, at[0]] = turn(found[0] * score_scale, tables, -1.0).astype(BF)
        lin_ref[:, at[1]] = turn(found[1] * score_scale, tables, -1.0).astype(BF)
        lin_ref[:, at[2]] = found[2].astype(BF)
    lin_own[...] = lin_ref[:rows]
    lin_sib[...] = lin_ref[rows:]
    sums_ref[...] = jnp.sum(lin_ref[...].astype(F32), axis=0, keepdims=True)
    for at, w in spans(weights):
        term = dot(lin_ref[...], w[:, : 3 * cols], 1, 1)
        mine_ref[:, at] = term[:rows].astype(BF)
        other_ref[:, at] = term[rows:].astype(BF)


def mlp_kernel(far, tiles, first, *refs):
    lines, grads, refs = refs[:2], refs[2:4], refs[4:]
    before, refs = (None, refs) if first else (refs[:2], refs[2:])
    weights, refs = refs[: far * tiles], refs[far * tiles :]
    found, sums, (held, held_grad) = refs[: 4 * tiles], refs[-4:-2], refs[-2:]
    rows = lines[0].shape[0]
    for half in range(2):
        here = slice(half * rows, (half + 1) * rows)
        held[here] = lines[half][...]
        held_grad[here] = grads[half][...]
    inner = []
    for t in range(tiles):
        mine = weights[t * far : (t + 1) * far]
        gate_up = sum(dot(held[:, at], w[:, : 2 * TILE], 1, 0) for at, w in spans(mine))
        hidden_grad = sum(dot(held_grad[:, at], w[:, 2 * TILE :], 1, 0) for at, w in spans(mine))
        gate_pre, up_values = gate_up[:, :TILE], gate_up[:, TILE:]
        gate_sig = jax.nn.sigmoid(gate_pre)
        smooth = gate_pre * gate_sig
        gate_grad = hidden_grad * up_values * gate_sig * (1.0 + gate_pre * (1.0 - gate_sig))
        hidden = (smooth * up_values).astype(BF)
        pair = jnp.concatenate([gate_grad.astype(BF), (hidden_grad * smooth).astype(BF)], axis=1)
        for half in range(2):
            here = slice(half * rows, (half + 1) * rows)
            found[4 * t + half][...] = pair[here]
            found[4 * t + 2 + half][...] = hidden[here]
        inner.append(pair)
    for p, (at, _) in enumerate(spans(weights[:far])):
        term = sum(
            dot(pair, weights[t * far + p][:, : 2 * TILE], 1, 1) for t, pair in enumerate(inner)
        )
        for half in range(2):
            part = term[half * rows : (half + 1) * rows]
            if not first:
                part = part + before[half][:, at]
            sums[half][:, at] = part.astype(sums[half].dtype)


def mlp_out_kernel(far, tiles, *refs):
    hiddens, refs = refs[: 2 * tiles], refs[2 * tiles :]
    weights, outs = refs[: far * tiles], refs[far * tiles :]
    for half in range(2):
        for p, (at, _) in enumerate(spans(weights[:far])):
            term = sum(
                dot(hiddens[2 * t + half][...], weights[t * far + p][...], 1, 1)
                for t in range(tiles)
            )
            outs[half][:, at] = term.astype(outs[half].dtype)


def grad_kernel(kinds, adds, *refs):
    lefts, rights = [], []
    at = 0
    for count in kinds:
        lefts.append(refs[at : at + 2])
        rights.append([refs[at + 2 + 2 * c : at + 4 + 2 * c] for c in range(count)])
        at += 2 + 2 * count
    more, out = refs[at : at + len(adds)], refs[-1]
    start = 0
    for left, columns in zip(lefts, rights):
        for right in columns:
            here = slice(start, start + right[0].shape[1])
            start = here.stop
            total = sum(dot(a[...], b[...], 0, 0) for a, b in zip(left, right))
            for extra, first in zip(more, adds):
                if first <= here.start < first + extra.shape[1]:
                    total = total + extra[:, here.start - first : here.stop - first].astype(F32)
            out[:, here] = total.astype(BF)


def copies_kernel(local_ref, out_ref):
    for k in range(out_ref.shape[0]):
        out_ref[k] = local_ref[...]


def on_device(
    tokens,
    segment_ids,
    ln1_gain,
    ln1_bias,
    qkv_weight,
    qkv_bias,
    out_weight,
    ln2_gain,
    ln2_bias,
    gate_up_weight,
    down_weight,
    out_grad,
):
    dp_size = lax.axis_size("dp")
    bits = dp_size.bit_length() - 1
    me = lax.axis_index("dp")
    core = lax.axis_index("tensor")
    rows, width = tokens.shape
    seq_len = segment_ids.shape[0]
    group = 1 << len(GROUP_BITS)
    far_bits = [b for b in reversed(range(bits)) if b not in GROUP_BITS]
    masks = [
        sum(1 << b for i, b in enumerate(GROUP_BITS) if (k >> i) & 1) for k in range(group)
    ]
    my_bit = [(me >> b) & 1 for b in range(bits)]
    rank = sum(my_bit[b] << i for i, b in enumerate(GROUP_BITS))
    heads = qkv_bias.shape[1] // HD // group
    head_cols = heads * HD
    hidden_cols = deal(down_weight.shape[0], group)[0] + LANES

    def swap(array, mask):
        if mask == 0:
            return array
        return lax.ppermute(array, "dp", [(d, d ^ mask) for d in range(dp_size)])

    def sibling(array):
        return lax.ppermute(array, "tensor", [(0, 1), (1, 0)])

    order = [bits - 1 - b for b in reversed(far_bits)]
    order += [bits - 1 - b for b in reversed(GROUP_BITS)]

    def swapped(array, axis, bit):
        low, high = jnp.split(array, 2, axis)
        low, high = jnp.where(bit == 1, high, low), jnp.where(bit == 1, low, high)
        return jnp.concatenate([low, high], axis)

    def to_rel(array):
        lead = array.ndim - 1
        cut = array.reshape(array.shape[:-1] + (2,) * bits + (width // dp_size,))
        cut = cut.transpose(list(range(lead)) + [lead + o for o in order] + [lead + bits])
        for i, b in enumerate(reversed(far_bits)):
            cut = swapped(cut, lead + i, my_bit[b])
        return cut.reshape(array.shape)

    def from_rel(array):
        lead = array.ndim - 1
        cut = array.reshape(array.shape[:-1] + (2,) * bits + (width // dp_size,))
        for i, b in enumerate(reversed(far_bits)):
            cut = swapped(cut, lead + i, my_bit[b])
        back = [order.index(i) for i in range(bits)]
        cut = cut.transpose(list(range(lead)) + [lead + o for o in back] + [lead + bits])
        return cut.reshape(array.shape)

    block = width // dp_size
    shard_rows = group * block
    far = 1 << len(far_bits)
    bands = [
        [d for d in range(dp_size) if all((d ^ first) >> b & 1 == 0 for b in far_bits)]
        for first in range(dp_size)
        if all(first >> b & 1 == 0 for b in GROUP_BITS)
    ]

    def exchange(rows_by_rank):
        return lax.all_to_all(rows_by_rank, "dp", 0, 0, axis_index_groups=bands, tiled=True)

    def tie(value, *after):
        return lax.optimization_barrier((value, *after))[0]

    def pack(kernel, ins, cols):
        return call(
            functools.partial(kernel, group), ins, [shaped((shard_rows, cols), BF)], 0
        )[0]

    def gather(shard, after=(), after_own=()):
        pieces = [shard]
        for n, b in enumerate(far_bits):
            own = tie(shard, *(after_own if n else after))
            pieces = pieces + [swap(p, 1 << b) for p in [own] + pieces[1:]]
        return pieces

    def copies(local):
        return jnp.broadcast_to(local, (group,) + local.shape)

    def spread(copied, after=(), then=()):
        mine = exchange(tie(copied, *after))
        return mine, sibling(tie(mine, *then))

    def half(array):
        return array.reshape((-1,) + array.shape[2:])

    def by_block(array):
        return array.reshape((group, -1) + array.shape[1:])

    def merge(mine, other, after=()):
        other = sibling(tie(other, *after))
        return (by_block(mine).astype(F32) + by_block(other).astype(F32)).astype(BF)

    def collect(both, after=()):
        return jnp.sum(exchange(tie(both, *after)).astype(F32), axis=0)

    wide = sorted(range(1, far), key=lambda i: (-i.bit_length(), -i))

    def below(i):
        bits_left = range(i.bit_length(), len(far_bits))
        return [c for b in bits_left for c in below(i | 1 << b) + [i | 1 << b]]

    def block_grad(i, kinds, adds, after=(), cost=LONG):
        cols = sum(c[0].shape[1] for _, sets in kinds for c in sets)
        ins, specs = [], []
        for left, sets in kinds:
            ins += left
            specs += [pl.BlockSpec((v.shape[0], shard_rows), lambda *_: (0, i)) for v in left]
            for s in sets:
                ins += s
                specs += [whole(v.shape) for v in s]
        ins += [v for v, _ in adds]
        specs += [whole(v.shape) for v, _ in adds]
        ins[0] = tie(ins[0], *after)
        return call(
            functools.partial(grad_kernel, [len(s) for _, s in kinds], [at for _, at in adds]),
            ins,
            [shaped((shard_rows, cols), BF)],
            2 * group * seq_len * shard_rows * cols,
            in_specs=specs,
            cost=cost,
        )[0]

    def send(i, part):
        return swap(part, 1 << far_bits[i.bit_length() - 1])

    def parent(i):
        return i ^ 1 << i.bit_length() - 1

    def finish(kernel, came, shapes):
        return call(functools.partial(kernel, group), came, [shaped(s, F32) for s in shapes], 0)

    gains = to_rel(jnp.stack([ln1_gain, ln1_bias, ln2_gain, ln2_bias]))
    resid = to_rel(tokens).astype(F32)
    normed_in, normed_one, inv_one = norm_parts(resid, gains[0], gains[1])
    seq_local = normed_in.astype(BF)
    attn_pack = pack(pack_attn_kernel, [qkv_weight, out_weight], 4 * head_cols)
    attn_shard = exchange(attn_pack)
    segs = jnp.stack([swap(tie(segment_ids, attn_pack), m) for m in masks])
    segs = segs.reshape((2,) * len(GROUP_BITS) + segs.shape[1:])
    for i, b in enumerate(reversed(GROUP_BITS)):
        segs = swapped(segs, i, my_bit[b])
    segs = segs.reshape(group, seq_len)
    mlp_pack = pack(pack_mlp_kernel, [tie(gate_up_weight, attn_shard), down_weight], 3 * hidden_cols)
    mlp_shard = exchange(tie(mlp_pack, attn_shard))
    w_attn = gather(attn_shard)
    tiles = hidden_cols // TILE
    spots = jax.vmap(doc_positions)(segs)
    segs, spots = (jnp.where(core == 1, jnp.roll(v, rows, axis=1), v) for v in (segs, spots))
    index = jnp.arange(seq_len, dtype=jnp.int32)
    index = jnp.where(core == 1, jnp.roll(index, rows), index)
    allowed = (segs[:, :, None] == segs[:, None, :]) & (index[None, :] <= index[:, None])
    mask = jnp.where(allowed, 0.0, masked_score).astype(F32)
    dim = jnp.arange(LANES, dtype=jnp.int32) % HD
    pair = (dim % (ROT // 2)).astype(F32)
    speed = jnp.where(dim < ROT, rope_base ** (-2.0 * pair / ROT), 0.0)
    angles = spots.astype(F32)[..., None] * speed
    cosine, sine = jnp.cos(angles), jnp.sin(angles)
    lead = jnp.where(dim < ROT // 2, -sine, 0.0)
    tail = jnp.where((dim >= ROT // 2) & (dim < ROT), sine, 0.0)

    w_mlp = []
    after, after_own = [w_attn[1]], [w_attn[-1]]
    for t in range(tiles):
        shard = mlp_shard[:, t * 3 * TILE : (t + 1) * 3 * TILE]
        w_mlp.append(gather(shard, after, after_own))
        after, after_own = [w_mlp[t][1]], [w_mlp[t][2]]
    grad_local = to_rel(tie(out_grad))
    grad_copies = copies(grad_local)
    heard = spread(
        tie(copies(seq_local), grad_copies, cosine, lead, tail, mask),
        [mlp_shard] + w_attn[1:2] + w_attn[2:3],
        w_attn[3:] + w_mlp[0][1:2],
    )
    seq_in = [half(h) for h in heard]
    grad_rows = spread(grad_copies, [heard[0]])

    bias = lax.dynamic_slice_in_dim(qkv_bias, rank * head_cols, head_cols, 1).reshape(1, -1)
    facts = [mask, cosine, lead, tail]
    lines = pltpu.VMEM((seq_len, width), BF)
    mine, other = shaped((group * rows, width), F32), shaped((group * rows, width), BF)
    term3 = shaped((group, rows, width), BF)
    qkv_shape = shaped((group, seq_len, 3 * head_cols), BF)
    mixed_shape = shaped((group, rows, head_cols), BF)
    lin_shape = shaped((group, rows, 3 * head_cols), BF)
    attn_flops = 2 * group * seq_len * width * 4 * head_cols

    ins = [*heard, bias] + facts + w_attn
    outs = [qkv_shape, mixed_shape, mixed_shape, term3, term3]
    qkv, mixed_own, mixed_sib, *terms = call(
        functools.partial(attend_kernel, len(w_attn)),
        ins,
        outs,
        attn_flops,
        in_specs=[each(v.shape) for v in heard]
        + [whole(bias.shape)]
        + [each(v.shape) for v in facts]
        + [whole(v.shape) for v in w_attn],
        out_specs=[each(v.shape) for v in outs],
        grid=(group,),
        scratch=[lines, pltpu.VMEM((seq_len, head_cols), BF)],
    )
    mixed = [half(mixed_own), half(mixed_sib)]
    both = merge(*map(half, terms), w_mlp[0][2:3] + [])
    attn_sum = collect(both, [grad_rows[0]] + [])
    resid_two = resid + tie(
        attn_sum, *w_mlp[0][3:], *w_mlp[1][1:2], *w_mlp[1][2:3]
    )
    normed_mid, normed_two, inv_two = norm_parts(resid_two, gains[2], gains[3])
    seq_mid = [half(h) for h in spread(copies(normed_mid.astype(BF)), (), w_mlp[1][3:] + w_mlp[2][1:2] + w_mlp[2][2:3])]
    grad_rows = [half(h) for h in grad_rows]

    row_spec = pl.BlockSpec((rows, width), lambda k: (k, 0))
    pair_spec, hidden_spec = (pl.BlockSpec((rows, n * TILE), lambda k: (k, 0)) for n in (2, 1))
    pair_shape, hidden_shape = (shaped((group * rows, n * TILE), BF) for n in (2, 1))
    weights = [[w for w in [mlp_shard] + w_mlp[t][1:]] for t in range(tiles)]
    inner, mid = [], []
    for batch in (range(tiles - 1), range(tiles - 1, tiles)):
        ins = [*seq_mid, *grad_rows] + mid
        final = batch[-1] == tiles - 1
        *found, mid_own, mid_sib = call(
            functools.partial(mlp_kernel, far, len(batch), not mid),
            ins + [w for t in batch for w in weights[t]],
            ([pair_shape] * 2 + [hidden_shape] * 2) * len(batch) + [other if final else mine] * 2,
            10 * group * seq_len * width * TILE * len(batch),
            in_specs=[row_spec] * len(ins)
            + [
                pl.BlockSpec((w.shape[0], 3 * TILE), lambda *_, t=0 if n else t: (0, t))
                for t in batch
                for n, w in enumerate(weights[t])
            ],
            out_specs=([pair_spec] * 2 + [hidden_spec] * 2) * len(batch) + [row_spec] * 2,
            grid=(group,),
            scratch=[lines, lines],
        )
        inner += found
        mid = [mid_own, mid_sib]
    weights = [w for ws in weights for w in ws]
    hiddens = [inner[4 * t + 2 : 4 * t + 4] for t in range(tiles)]
    tile_kinds = [
        [(seq_mid, [inner[4 * t : 4 * t + 2]]), (grad_rows, [hiddens[t]])] for t in range(tiles)
    ]
    all_kinds = [kind for kinds in tile_kinds for kind in kinds]
    both = merge(mid_own, mid_sib)

    last = far // 2
    batches = [range(t, t + 1) for t in range(tiles)]
    batch_kinds = [[kind for t in batch for kind in tile_kinds[t]] for batch in batches]
    batch_adds = [[[] for _ in range(far)] for _ in batches]
    first_parts, first_came, later, later_came, held = [], [], [], [], []

    def batch_step(n, i, after):
        part = block_grad(i, batch_kinds[n], [(v, 0) for v in batch_adds[n][i]], after)
        if i == 1 and n >= 2:
            held.append((n, i, part))
            return part, None
        came = send(i, part)
        batch_adds[n][parent(i)].append(came)
        return part, came

    steps = [i for i in below(0) if i != last]
    for n in range(len(batches)):
        part, came = batch_step(n, steps[0], [both] + first_parts if n else [])
        first_parts.append(part)
        first_came.append(came)
    last_part = block_grad(last, all_kinds, [], first_parts, cost=LONG)
    last_came = send(last, last_part)
    mid_local = tie(collect(both), last_part, *first_came[:1])
    resid_grad = grad_local.astype(F32) + norm_back(mid_local, normed_two, inv_two, gains[2])
    resid_back = resid_grad.astype(BF)
    copied = copies(resid_back)
    for i in steps[1:]:
        for n in range(len(batches)):
            part, came = batch_step(n, i, [copied] + later)
            later.append(part)
            later_came.append(came)
    out_ins = [h for pair in hiddens for h in pair]
    out_ins[0] = tie(out_ins[0], copied)
    out_terms = call(
        functools.partial(mlp_out_kernel, far, tiles),
        out_ins + weights,
        [other, other],
        2 * group * seq_len * width * hidden_cols,
        in_specs=[whole(v.shape) for v in out_ins]
        + [
            pl.BlockSpec((w.shape[0], TILE), lambda *_, t=3 * (n // far) if n % far == 0 else 0: (0, t + 2))
            for n, w in enumerate(weights)
        ],
        cost=SHORT,
    )
    out_both = merge(*out_terms)
    attn_grad = spread(copied, [], [out_both] + later + later_came[:1] + [])
    ins = [*attn_grad, qkv] + facts + w_attn
    outs = [lin_shape, lin_shape, shaped((group, 1, 3 * head_cols), F32), term3, term3]
    lin_own, lin_sib, bias_sums, *terms = call(
        functools.partial(attend_back_kernel, len(w_attn)),
        ins,
        outs,
        attn_flops,
        in_specs=[each(v.shape) for v in ins[: 3 + len(facts)]] + [whole(v.shape) for v in w_attn],
        out_specs=[each(v.shape) for v in outs],
        grid=(group,),
        scratch=[lines, pltpu.VMEM((seq_len, 3 * head_cols), BF)],
    )
    bias_sums = jnp.sum(bias_sums, axis=(0, 1))
    for n, i, part in held:
        came = send(i, tie(part, lin_own))
        batch_adds[n][parent(i)].append(came)
        later_came.append(came)
    later_came = [came for came in later_came if came is not None]
    both = merge(*map(half, terms), [])
    out_sum = collect(out_both, [attn_grad[0]])
    in_grad = tie(collect(both, [out_sum]), *later_came[2:3])
    attn_kinds = [
        (seq_in, [[half(lin_own), half(lin_sib)]]),
        ([half(h) for h in attn_grad], [mixed]),
    ]
    attn_adds = [[] for _ in range(far)]
    parts, attn_sent = [], []
    for n, i in enumerate(wide):
        after = (([] + parts) if attn_adds[i] else [both] + parts) if n else []
        part = block_grad(i, attn_kinds, [(v, 0) for v in attn_adds[i]], after)
        parts.append(part)
        attn_sent.append(send(i, part))
        attn_adds[parent(i)].append(attn_sent[-1])
    token_grad = from_rel(resid_grad + norm_back(in_grad, normed_one, inv_one, gains[0]))

    def sum_all(array):
        array = array + sibling(array)
        yield sum((swap(array, m) for m in masks[1:]), array)

    def far_sum(array):
        for at in range(0, len(far_bits), 2):
            pair = [1 << b for b in far_bits[at : at + 2]]
            array = sum((swap(array, m) for m in pair + [sum(pair)][: len(pair) - 1]), array)
        return array

    def both_sums(grad, normed):
        return [jnp.sum(grad * normed, axis=0), jnp.sum(grad, axis=0)]

    norm_sums = jnp.stack(both_sums(in_grad, normed_one) + both_sums(mid_local, normed_two))
    bias_full = lax.dynamic_update_slice(
        jnp.zeros((3, head_cols * group * lax.axis_size("tensor")), F32),
        bias_sums.reshape(3, head_cols),
        (jnp.int32(0), (core * group + rank) * head_cols),
    )
    sums = list(sum_all(jnp.concatenate([from_rel(norm_sums), bias_full])))
    sums.append(far_sum(sums[0]))
    result = from_rel((resid_two + out_sum).astype(BF))
    adds = [(v, 3 * TILE * b[0]) for b, into in zip(batches, batch_adds) for v in into[0]]
    adds.append((last_came, 0))
    mlp_after = parts
    mlp_mine = block_grad(0, all_kinds, adds, mlp_after)
    attn_after = sums[1:] + [result]
    attn_mine = block_grad(0, attn_kinds, [(v, 0) for v in attn_adds[0]], attn_after)
    mlp_came = exchange(tie(mlp_mine, in_grad, out_sum))
    attn_came = exchange(tie(attn_mine, mlp_came))
    gate_up_grad, down_grad = finish(
        finish_mlp_kernel, [mlp_came], (gate_up_weight.shape, down_weight.shape)
    )
    qkv_grad, out_w_grad = finish(
        finish_attn_kernel, [attn_came], (qkv_weight.shape, out_weight.shape)
    )
    sums = sums[-1]
    return (
        result,
        token_grad,
        sums[0],
        sums[1],
        qkv_grad,
        sums[4:],
        out_w_grad,
        sums[2],
        sums[3],
        gate_up_grad,
        down_grad,
    )


def solution(mesh):
    return jax.shard_map(
        on_device,
        mesh=mesh,
        in_specs=(
            P(("dp", "tensor"), None),
            P("dp"),
            P(),
            P(),
            P(None, "dp", "tensor"),
            P(None, "tensor"),
            P("tensor", "dp"),
            P(),
            P(),
            P(None, "dp", "tensor"),
            P("tensor", "dp"),
            P(("dp", "tensor"), None),
        ),
        out_specs=(
            P(("dp", "tensor"), None),
            P(("dp", "tensor"), None),
            P(),
            P(),
            P(None, "dp", "tensor"),
            P(),
            P("tensor", "dp"),
            P(),
            P(),
            P(None, "dp", "tensor"),
            P("tensor", "dp"),
        ),
        check_vma=False,
    )
```

```python
import functools

import jax
import jax.numpy as jnp
from jax import lax
from jax.experimental import pallas as pl
from jax.experimental.pallas import tpu as pltpu
from jax.sharding import PartitionSpec as P

HD = 64
ROT = 16
LANES = 128

norm_eps = 1e-05
rope_base = 10000.0
score_scale = 0.125
masked_score = -1e30

GROUP_BITS = (1, 2)
BF = jnp.bfloat16
F32 = jnp.float32
VMEM_LIMIT = 60 * 1024 * 1024


def norm_parts(values, gain, shift):
    row_mean = jnp.mean(values, axis=-1, keepdims=True)
    centred = values - row_mean
    inv_std = lax.rsqrt(jnp.mean(centred * centred, axis=-1, keepdims=True) + norm_eps)
    normed = centred * inv_std
    return (normed * gain + shift, normed, inv_std)


def norm_back(incoming, normed, inv_std, gain):
    scaled = incoming * gain
    adjusted = (
        scaled
        - jnp.mean(scaled, axis=-1, keepdims=True)
        - normed * jnp.mean(scaled * normed, axis=-1, keepdims=True)
    )
    return adjusted * inv_std


def dot(a, b, a_dim, b_dim):
    return lax.dot_general(
        a, b, (((a_dim,), (b_dim,)), ((), ())), preferred_element_type=F32
    )


def whole(shape, once=False):
    zeros = (0,) * len(shape)
    return pl.BlockSpec(
        shape, lambda *_: zeros, pipeline_mode=pl.Buffered(buffer_count=1) if once else None
    )


def each(shape):
    zeros = (0,) * (len(shape) - 1)
    return pl.BlockSpec((None,) + shape[1:], lambda k, *_: (k,) + zeros)


LONG, SHORT = 30, 0


def call(
    kernel, ins, out_shapes, flops, in_specs=None, out_specs=None, grid=(1,), scratch=(), cost=LONG
):
    moved = cost * sum(v.size * v.dtype.itemsize for v in [*ins, *out_shapes])
    return pl.pallas_call(
        kernel,
        grid=grid,
        in_specs=in_specs or [whole(v.shape) for v in ins],
        out_specs=out_specs or [whole(s.shape) for s in out_shapes],
        out_shape=list(out_shapes),
        scratch_shapes=list(scratch),
        compiler_params=pltpu.CompilerParams(vmem_limit_bytes=VMEM_LIMIT),
        cost_estimate=pl.CostEstimate(flops=cost * flops, bytes_accessed=moved, transcendentals=0),
    )(*ins)


def shaped(shape, dtype):
    return jax.ShapeDtypeStruct(shape, dtype)


def deal(cols, group):
    full = cols // (LANES * group) * LANES
    share = (cols - full * group) // group
    return full, share


def pack_attn_kernel(group, qkv_ref, out_ref, sent_ref):
    cols = qkv_ref.shape[2] // group
    block = qkv_ref.shape[1]
    for k in range(group):
        at, here = slice(k * cols, (k + 1) * cols), slice(k * block, (k + 1) * block)
        for j in range(3):
            sent_ref[here, j * cols : (j + 1) * cols] = qkv_ref[j, :, at]
        sent_ref[here, 3 * cols :] = out_ref[at, :].T


TILE = 2 * LANES


def column(j, at):
    return at // TILE * 3 * TILE + j * TILE + at % TILE


def pack_mlp_kernel(group, gate_up_ref, down_ref, sent_ref):
    full, share = deal(gate_up_ref.shape[2], group)
    block = gate_up_ref.shape[1]
    per = LANES // share
    lane = lax.broadcasted_iota(jnp.int32, (1, LANES), 1) // share
    for k in range(group):
        here = slice(k * block, (k + 1) * block)
        for at in range(0, full + LANES, LANES):
            own = at < full
            start = k * full + at if own else group * full + k // per * LANES
            take = slice(start, start + LANES)
            for j in range(3):
                value = gate_up_ref[j, :, take] if j < 2 else down_ref[take, :].T
                if not own:
                    value = jnp.where(lane == k % per, value, 0).astype(BF)
                to = column(j, at)
                sent_ref[here, to : to + LANES] = value


def finish_mlp_kernel(group, *refs):
    got, gate_up_ref, down_ref = refs
    full, share = deal(gate_up_ref.shape[2], group)
    block = gate_up_ref.shape[1]
    per = LANES // share

    def taken(k, j, at):
        to = column(j, at)
        return got[k * block : (k + 1) * block, to : to + LANES].astype(F32)

    for j in range(3):
        for at in range(0, full + LANES, LANES):
            own = at < full
            for k in range(0, group, 1 if own else per):
                start = k * full + at if own else group * full + k // per * LANES
                take = slice(start, start + LANES)
                value = sum(taken(k + i, j, at) for i in range(1 if own else per))
                if j < 2:
                    gate_up_ref[j, :, take] = value
                else:
                    down_ref[take, :] = value.T


def finish_attn_kernel(group, got_ref, qkv_ref, out_ref):
    cols = qkv_ref.shape[2] // group
    block = qkv_ref.shape[1]
    for k in range(group):
        here, at = slice(k * block, (k + 1) * block), slice(k * cols, (k + 1) * cols)
        for j in range(3):
            qkv_ref[j, :, at] = got_ref[here, j * cols : (j + 1) * cols].astype(F32)
        out_ref[at, :] = got_ref[here, 3 * cols :].astype(F32).T


def spans(weights):
    at = 0
    for w in weights:
        yield slice(at, at + w.shape[0]), w
        at += w.shape[0]


def turn(value, tables, sign):
    cosine, lead, tail = tables
    ahead = pltpu.roll(value, LANES - ROT // 2, 1)
    behind = pltpu.roll(value, ROT // 2, 1)
    return value * cosine + (ahead * lead + behind * tail) * sign


def soft(left, right, mask, axis):
    scores = dot(left, right, 1, 1) * score_scale + mask
    weights = jnp.exp(scores - jnp.max(scores, axis=axis, keepdims=True))
    return weights * (1.0 / jnp.sum(weights, axis=axis, keepdims=True))


def own_head(half):
    return lax.broadcasted_iota(jnp.int32, (1, LANES), 1) // HD == half


def attend_kernel(far, own_ref, sib_ref, bias_ref, mask_ref, cos_ref, lead_ref, tail_ref, *refs):
    weights, refs = refs[:far], refs[far:]
    qkv_ref, mixed_own, mixed_sib, mine_ref, other_ref, lines, mixed_ref = refs
    rows = mine_ref.shape[0]
    lines[:rows] = own_ref[...]
    lines[rows:] = sib_ref[...]
    cols = mixed_ref.shape[1]
    tables = (cos_ref[...], lead_ref[...], tail_ref[...])
    lin = bias_ref[...]
    for at, w in spans(weights):
        lin = lin + dot(lines[:, at], w[:, : 3 * cols], 1, 0)
    mask = mask_ref[...]
    for i in range(cols // LANES):
        at = [slice(j * cols + i * LANES, j * cols + (i + 1) * LANES) for j in range(3)]
        queries = turn(lin[:, at[0]], tables, 1.0).astype(BF)
        keys = turn(lin[:, at[1]], tables, 1.0).astype(BF)
        values = lin[:, at[2]].astype(BF)
        qkv_ref[:, at[0]] = queries
        qkv_ref[:, at[1]] = keys
        qkv_ref[:, at[2]] = values
        mixed = None
        for half in range(LANES // HD):
            here = own_head(half)
            probs = soft(jnp.where(here, queries, 0).astype(BF), keys, mask, 1).astype(BF)
            part = dot(probs, values, 1, 0)
            mixed = part if mixed is None else jnp.where(here, part, mixed)
        mixed_ref[:, i * LANES : (i + 1) * LANES] = mixed.astype(BF)
    mixed_own[...] = mixed_ref[:rows]
    mixed_sib[...] = mixed_ref[rows:]
    for at, w in spans(weights):
        term = dot(mixed_ref[...], w[:, 3 * cols :], 1, 1)
        mine_ref[:, at] = term[:rows].astype(BF)
        other_ref[:, at] = term[rows:].astype(BF)


def attend_back_kernel(far, own_ref, sib_ref, qkv_ref, mask_ref, cos_ref, lead_ref, tail_ref, *refs):
    weights, refs = refs[:far], refs[far:]
    lin_own, lin_sib, sums_ref, mine_ref, other_ref, lines, lin_ref = refs
    rows = own_ref.shape[0]
    lines[:rows] = own_ref[...]
    lines[rows:] = sib_ref[...]
    cols = qkv_ref.shape[1] // 3
    tables = (cos_ref[...], lead_ref[...], tail_ref[...])
    mixed_grad = sum(dot(lines[:, at], w[:, 3 * cols :], 1, 0) for at, w in spans(weights))
    mixed_grad = mixed_grad.astype(BF)
    mask = mask_ref[...]
    for i in range(cols // LANES):
        at = [slice(j * cols + i * LANES, j * cols + (i + 1) * LANES) for j in range(3)]
        queries, keys, values = (qkv_ref[:, a] for a in at)
        grad = mixed_grad[:, i * LANES : (i + 1) * LANES]
        found = [None] * 3
        for half in range(LANES // HD):
            here = own_head(half)
            probs = soft(keys, jnp.where(here, queries, 0).astype(BF), mask, 0)
            value_grad = dot(probs.astype(BF), grad, 1, 0)
            prob_grad = dot(values, jnp.where(here, grad, 0).astype(BF), 1, 1)
            score_grad = (
                probs * (prob_grad - jnp.sum(probs * prob_grad, axis=0, keepdims=True))
            ).astype(BF)
            query_grad = dot(score_grad, keys, 0, 0)
            key_grad = dot(score_grad, queries, 1, 0)
            parts = (query_grad, key_grad, value_grad)
            found = [p if f is None else jnp.where(here, p, f) for p, f in zip(parts, found)]
        lin_ref[:, at[0]] = turn(found[0] * score_scale, tables, -1.0).astype(BF)
        lin_ref[:, at[1]] = turn(found[1] * score_scale, tables, -1.0).astype(BF)
        lin_ref[:, at[2]] = found[2].astype(BF)
    lin_own[...] = lin_ref[:rows]
    lin_sib[...] = lin_ref[rows:]
    sums_ref[...] = jnp.sum(lin_ref[...].astype(F32), axis=0, keepdims=True)
    for at, w in spans(weights):
        term = dot(lin_ref[...], w[:, : 3 * cols], 1, 1)
        mine_ref[:, at] = term[:rows].astype(BF)
        other_ref[:, at] = term[rows:].astype(BF)


def mlp_kernel(far, tiles, first, *refs):
    lines, grads, refs = refs[:2], refs[2:4], refs[4:]
    before, refs = (None, refs) if first else (refs[:2], refs[2:])
    weights, refs = refs[: far * tiles], refs[far * tiles :]
    found, sums, (held, held_grad) = refs[: 4 * tiles], refs[-4:-2], refs[-2:]
    rows = lines[0].shape[0]
    for half in range(2):
        here = slice(half * rows, (half + 1) * rows)
        held[here] = lines[half][...]
        held_grad[here] = grads[half][...]
    inner = []
    for t in range(tiles):
        mine = weights[t * far : (t + 1) * far]
        gate_up = sum(dot(held[:, at], w[:, : 2 * TILE], 1, 0) for at, w in spans(mine))
        hidden_grad = sum(dot(held_grad[:, at], w[:, 2 * TILE :], 1, 0) for at, w in spans(mine))
        gate_pre, up_values = gate_up[:, :TILE], gate_up[:, TILE:]
        gate_sig = jax.nn.sigmoid(gate_pre)
        smooth = gate_pre * gate_sig
        gate_grad = hidden_grad * up_values * gate_sig * (1.0 + gate_pre * (1.0 - gate_sig))
        hidden = (smooth * up_values).astype(BF)
        pair = jnp.concatenate([gate_grad.astype(BF), (hidden_grad * smooth).astype(BF)], axis=1)
        for half in range(2):
            here = slice(half * rows, (half + 1) * rows)
            found[4 * t + half][...] = pair[here]
            found[4 * t + 2 + half][...] = hidden[here]
        inner.append(pair)
    for p, (at, _) in enumerate(spans(weights[:far])):
        term = sum(
            dot(pair, weights[t * far + p][:, : 2 * TILE], 1, 1) for t, pair in enumerate(inner)
        )
        for half in range(2):
            part = term[half * rows : (half + 1) * rows]
            if not first:
                part = part + before[half][:, at]
            sums[half][:, at] = part.astype(sums[half].dtype)


def mlp_out_kernel(far, tiles, *refs):
    hiddens, refs = refs[: 2 * tiles], refs[2 * tiles :]
    weights, outs = refs[: far * tiles], refs[far * tiles :]
    for half in range(2):
        for p, (at, _) in enumerate(spans(weights[:far])):
            term = sum(
                dot(hiddens[2 * t + half][...], weights[t * far + p][...], 1, 1)
                for t in range(tiles)
            )
            outs[half][:, at] = term.astype(outs[half].dtype)


def grad_kernel(kinds, adds, *refs):
    lefts, rights = [], []
    at = 0
    for count in kinds:
        lefts.append(refs[at : at + 2])
        rights.append([refs[at + 2 + 2 * c : at + 4 + 2 * c] for c in range(count)])
        at += 2 + 2 * count
    more, out = refs[at : at + len(adds)], refs[-1]
    start = 0
    for left, columns in zip(lefts, rights):
        for right in columns:
            here = slice(start, start + right[0].shape[1])
            start = here.stop
            total = sum(dot(a[...], b[...], 0, 0) for a, b in zip(left, right))
            for extra, first in zip(more, adds):
                if first <= here.start < first + extra.shape[1]:
                    total = total + extra[:, here.start - first : here.stop - first].astype(F32)
            out[:, here] = total.astype(BF)


def copies_kernel(local_ref, out_ref):
    for k in range(out_ref.shape[0]):
        out_ref[k] = local_ref[...]


def on_device(
    tokens,
    segment_ids,
    ln1_gain,
    ln1_bias,
    qkv_weight,
    qkv_bias,
    out_weight,
    ln2_gain,
    ln2_bias,
    gate_up_weight,
    down_weight,
    out_grad,
):
    dp_size = lax.axis_size("dp")
    bits = dp_size.bit_length() - 1
    me = lax.axis_index("dp")
    core = lax.axis_index("tensor")
    rows, width = tokens.shape
    seq_len = segment_ids.shape[0]
    group = 1 << len(GROUP_BITS)
    far_bits = [b for b in reversed(range(bits)) if b not in GROUP_BITS]
    masks = [
        sum(1 << b for i, b in enumerate(GROUP_BITS) if (k >> i) & 1) for k in range(group)
    ]
    my_bit = [(me >> b) & 1 for b in range(bits)]
    rank = sum(my_bit[b] << i for i, b in enumerate(GROUP_BITS))
    heads = qkv_bias.shape[1] // HD // group
    head_cols = heads * HD
    hidden_cols = deal(down_weight.shape[0], group)[0] + LANES

    def swap(array, mask):
        if mask == 0:
            return array
        return lax.ppermute(array, "dp", [(d, d ^ mask) for d in range(dp_size)])

    def sibling(array):
        return lax.ppermute(array, "tensor", [(0, 1), (1, 0)])

    order = [bits - 1 - b for b in reversed(far_bits)]
    order += [bits - 1 - b for b in reversed(GROUP_BITS)]

    def swapped(array, axis, bit):
        low, high = jnp.split(array, 2, axis)
        low, high = jnp.where(bit == 1, high, low), jnp.where(bit == 1, low, high)
        return jnp.concatenate([low, high], axis)

    def to_rel(array):
        lead = array.ndim - 1
        cut = array.reshape(array.shape[:-1] + (2,) * bits + (width // dp_size,))
        cut = cut.transpose(list(range(lead)) + [lead + o for o in order] + [lead + bits])
        for i, b in enumerate(reversed(far_bits)):
            cut = swapped(cut, lead + i, my_bit[b])
        return cut.reshape(array.shape)

    def from_rel(array):
        lead = array.ndim - 1
        cut = array.reshape(array.shape[:-1] + (2,) * bits + (width // dp_size,))
        for i, b in enumerate(reversed(far_bits)):
            cut = swapped(cut, lead + i, my_bit[b])
        back = [order.index(i) for i in range(bits)]
        cut = cut.transpose(list(range(lead)) + [lead + o for o in back] + [lead + bits])
        return cut.reshape(array.shape)

    block = width // dp_size
    shard_rows = group * block
    far = 1 << len(far_bits)
    bands = [
        [d for d in range(dp_size) if all((d ^ first) >> b & 1 == 0 for b in far_bits)]
        for first in range(dp_size)
        if all(first >> b & 1 == 0 for b in GROUP_BITS)
    ]

    def exchange(rows_by_rank):
        return lax.all_to_all(rows_by_rank, "dp", 0, 0, axis_index_groups=bands, tiled=True)

    def tie(value, *after):
        return lax.optimization_barrier((value, *after))[0]

    def pack(kernel, ins, cols):
        return call(
            functools.partial(kernel, group), ins, [shaped((shard_rows, cols), BF)], 0
        )[0]

    def gather(shard, after=(), after_own=()):
        pieces = [shard]
        for n, b in enumerate(far_bits):
            own = tie(shard, *(after_own if n else after))
            pieces = pieces + [swap(p, 1 << b) for p in [own] + pieces[1:]]
        return pieces

    def copies(local):
        return jnp.broadcast_to(local, (group,) + local.shape)

    def spread(copied, after=(), then=()):
        mine = exchange(tie(copied, *after))
        return mine, sibling(tie(mine, *then))

    def half(array):
        return array.reshape((-1,) + array.shape[2:])

    def by_block(array):
        return array.reshape((group, -1) + array.shape[1:])

    def merge(mine, other, after=()):
        other = sibling(tie(other, *after))
        return (by_block(mine).astype(F32) + by_block(other).astype(F32)).astype(BF)

    def collect(both, after=()):
        return jnp.sum(exchange(tie(both, *after)).astype(F32), axis=0)

    wide = sorted(range(1, far), key=lambda i: (-i.bit_length(), -i))

    def below(i):
        bits_left = range(i.bit_length(), len(far_bits))
        return [c for b in bits_left for c in below(i | 1 << b) + [i | 1 << b]]

    def block_grad(i, kinds, adds, after=(), cost=LONG):
        cols = sum(c[0].shape[1] for _, sets in kinds for c in sets)
        ins, specs = [], []
        for left, sets in kinds:
            ins += left
            specs += [pl.BlockSpec((v.shape[0], shard_rows), lambda *_: (0, i)) for v in left]
            for s in sets:
                ins += s
                specs += [whole(v.shape) for v in s]
        ins += [v for v, _ in adds]
        specs += [whole(v.shape) for v, _ in adds]
        ins[0] = tie(ins[0], *after)
        return call(
            functools.partial(grad_kernel, [len(s) for _, s in kinds], [at for _, at in adds]),
            ins,
            [shaped((shard_rows, cols), BF)],
            2 * group * seq_len * shard_rows * cols,
            in_specs=specs,
            cost=cost,
        )[0]

    def send(i, part):
        return swap(part, 1 << far_bits[i.bit_length() - 1])

    def parent(i):
        return i ^ 1 << i.bit_length() - 1

    def finish(kernel, came, shapes):
        return call(functools.partial(kernel, group), came, [shaped(s, F32) for s in shapes], 0)

    gains = to_rel(jnp.stack([ln1_gain, ln1_bias, ln2_gain, ln2_bias]))
    resid = to_rel(tokens).astype(F32)
    normed_in, normed_one, inv_one = norm_parts(resid, gains[0], gains[1])
    seq_local = normed_in.astype(BF)
    attn_pack = pack(pack_attn_kernel, [qkv_weight, out_weight], 4 * head_cols)
    attn_shard = exchange(attn_pack)
    segs = jnp.stack([swap(tie(segment_ids, attn_pack), m) for m in masks])
    segs = segs.reshape((2,) * len(GROUP_BITS) + segs.shape[1:])
    for i, b in enumerate(reversed(GROUP_BITS)):
        segs = swapped(segs, i, my_bit[b])
    segs = segs.reshape(group, seq_len)
    mlp_pack = pack(pack_mlp_kernel, [tie(gate_up_weight, attn_shard), down_weight], 3 * hidden_cols)
    mlp_shard = exchange(tie(mlp_pack, attn_shard))
    w_attn = gather(attn_shard)
    tiles = hidden_cols // TILE
    segs = tie(segs, w_attn[2])
    segs = jnp.where(core == 1, jnp.roll(segs, rows, axis=1), segs)
    index = jnp.arange(seq_len, dtype=jnp.int32)
    index = jnp.where(core == 1, jnp.roll(index, rows), index)
    spots = index - jnp.sum(segs[:, None, :] < segs[:, :, None], axis=2, dtype=jnp.int32)
    allowed = (segs[:, :, None] == segs[:, None, :]) & (index[None, :] <= index[:, None])
    mask = jnp.where(allowed, 0.0, masked_score).astype(F32)
    allowed_back = (segs[:, :, None] == segs[:, None, :]) & (index[None, :] >= index[:, None])
    mask_back = jnp.where(allowed_back, 0.0, masked_score).astype(F32)
    dim = jnp.arange(LANES, dtype=jnp.int32) % HD
    pair = (dim % (ROT // 2)).astype(F32)
    speed = jnp.where(dim < ROT, rope_base ** (-2.0 * pair / ROT), 0.0)
    angles = spots.astype(F32)[..., None] * speed
    cosine, sine = jnp.cos(angles), jnp.sin(angles)
    lead = jnp.where(dim < ROT // 2, -sine, 0.0)
    tail = jnp.where((dim >= ROT // 2) & (dim < ROT), sine, 0.0)

    w_mlp = []
    after, after_own = [w_attn[1]], [w_attn[-1]]
    for t in range(tiles):
        shard = mlp_shard[:, t * 3 * TILE : (t + 1) * 3 * TILE]
        w_mlp.append(gather(shard, after, after_own))
        after, after_own = [w_mlp[t][1]], [w_mlp[t][2]]
    grad_local = to_rel(tie(out_grad, w_attn[2]))
    grad_copies = copies(grad_local)
    heard = spread(
        tie(copies(seq_local), grad_copies, cosine, lead, tail, mask),
        [mlp_shard] + w_attn[1:2] + w_attn[2:3],
        w_attn[3:] + w_mlp[0][1:2],
    )
    seq_in = [half(h) for h in heard]
    grad_rows = spread(grad_copies, [heard[0]])

    bias = lax.dynamic_slice_in_dim(qkv_bias, rank * head_cols, head_cols, 1).reshape(1, -1)
    facts = [mask, cosine, lead, tail]
    lines = pltpu.VMEM((seq_len, width), BF)
    mine, other = shaped((group * rows, width), F32), shaped((group * rows, width), BF)
    term3 = shaped((group, rows, width), BF)
    qkv_shape = shaped((group, seq_len, 3 * head_cols), BF)
    mixed_shape = shaped((group, rows, head_cols), BF)
    lin_shape = shaped((group, rows, 3 * head_cols), BF)
    attn_flops = 2 * group * seq_len * width * 4 * head_cols

    ins = [*heard, bias] + facts + w_attn
    outs = [qkv_shape, mixed_shape, mixed_shape, term3, term3]
    qkv, mixed_own, mixed_sib, *terms = call(
        functools.partial(attend_kernel, len(w_attn)),
        ins,
        outs,
        attn_flops,
        in_specs=[each(v.shape) for v in heard]
        + [whole(bias.shape)]
        + [each(v.shape) for v in facts]
        + [whole(v.shape) for v in w_attn],
        out_specs=[each(v.shape) for v in outs],
        grid=(group,),
        scratch=[lines, pltpu.VMEM((seq_len, head_cols), BF)],
    )
    mixed = [half(mixed_own), half(mixed_sib)]
    both = merge(*map(half, terms), w_mlp[0][2:3])
    attn_sum = collect(both, [grad_rows[0]])
    resid_two = resid + tie(
        attn_sum, *w_mlp[0][3:], *w_mlp[1][1:2], *w_mlp[1][2:3]
    )
    normed_mid, normed_two, inv_two = norm_parts(resid_two, gains[2], gains[3])
    seq_mid = [half(h) for h in spread(copies(normed_mid.astype(BF)), (), w_mlp[1][3:] + w_mlp[2][1:2] + w_mlp[2][2:3])]
    grad_rows = [half(h) for h in grad_rows]

    row_spec = pl.BlockSpec((rows, width), lambda k: (k, 0))
    pair_spec, hidden_spec = (pl.BlockSpec((rows, n * TILE), lambda k: (k, 0)) for n in (2, 1))
    pair_shape, hidden_shape = (shaped((group * rows, n * TILE), BF) for n in (2, 1))
    weights = [[w for w in [mlp_shard] + w_mlp[t][1:]] for t in range(tiles)]
    inner, mid = [], []
    for batch in (range(tiles - 1), range(tiles - 1, tiles)):
        ins = [*seq_mid, *grad_rows] + mid
        final = batch[-1] == tiles - 1
        *found, mid_own, mid_sib = call(
            functools.partial(mlp_kernel, far, len(batch), not mid),
            ins + [w for t in batch for w in weights[t]],
            ([pair_shape] * 2 + [hidden_shape] * 2) * len(batch) + [other if final else mine] * 2,
            10 * group * seq_len * width * TILE * len(batch),
            in_specs=[row_spec] * len(ins)
            + [
                pl.BlockSpec((w.shape[0], 3 * TILE), lambda *_, t=0 if n else t: (0, t))
                for t in batch
                for n, w in enumerate(weights[t])
            ],
            out_specs=([pair_spec] * 2 + [hidden_spec] * 2) * len(batch) + [row_spec] * 2,
            grid=(group,),
            scratch=[lines, lines],
        )
        inner += found
        mid = [mid_own, mid_sib]
    weights = [w for ws in weights for w in ws]
    hiddens = [inner[4 * t + 2 : 4 * t + 4] for t in range(tiles)]
    tile_kinds = [
        [(seq_mid, [inner[4 * t : 4 * t + 2]]), (grad_rows, [hiddens[t]])] for t in range(tiles)
    ]
    all_kinds = [kind for kinds in tile_kinds for kind in kinds]
    both = merge(mid_own, mid_sib)

    last = far // 2
    batches = [range(t, t + 1) for t in range(tiles)]
    batch_kinds = [[kind for t in batch for kind in tile_kinds[t]] for batch in batches]
    batch_adds = [[[] for _ in range(far)] for _ in batches]
    first_parts, first_came, later, later_came, held = [], [], [], [], []

    def batch_step(n, i, after):
        part = block_grad(i, batch_kinds[n], [(v, 0) for v in batch_adds[n][i]], after)
        if i == 1 and n >= 2:
            held.append((n, i, part))
            return part, None
        came = send(i, part)
        batch_adds[n][parent(i)].append(came)
        return part, came

    steps = [i for i in below(0) if i != last]
    for n in range(len(batches)):
        part, came = batch_step(n, steps[0], [both] + first_parts if n else [])
        first_parts.append(part)
        first_came.append(came)
    last_part = block_grad(last, all_kinds, [], first_parts, cost=LONG)
    last_came = send(last, last_part)
    mid_local = tie(collect(both), last_part, *first_came[:1])
    resid_grad = grad_local.astype(F32) + norm_back(mid_local, normed_two, inv_two, gains[2])
    resid_back = resid_grad.astype(BF)
    copied = copies(resid_back)
    for i in steps[1:]:
        for n in range(len(batches)):
            part, came = batch_step(n, i, [copied] + later)
            later.append(part)
            later_came.append(came)
    out_ins = [h for pair in hiddens for h in pair]
    out_ins[0] = tie(out_ins[0], copied)
    out_terms = call(
        functools.partial(mlp_out_kernel, far, tiles),
        out_ins + weights,
        [other, other],
        2 * group * seq_len * width * hidden_cols,
        in_specs=[whole(v.shape) for v in out_ins]
        + [
            pl.BlockSpec((w.shape[0], TILE), lambda *_, t=3 * (n // far) if n % far == 0 else 0: (0, t + 2))
            for n, w in enumerate(weights)
        ],
        cost=SHORT,
    )
    out_both = merge(*out_terms)
    attn_grad = spread(copied, [], [out_both] + later + later_came[:1])
    ins = [*attn_grad, qkv, mask_back] + facts[1:] + w_attn
    outs = [lin_shape, lin_shape, shaped((group, 1, 3 * head_cols), F32), term3, term3]
    lin_own, lin_sib, bias_sums, *terms = call(
        functools.partial(attend_back_kernel, len(w_attn)),
        ins,
        outs,
        attn_flops,
        in_specs=[each(v.shape) for v in ins[: 3 + len(facts)]] + [whole(v.shape) for v in w_attn],
        out_specs=[each(v.shape) for v in outs],
        grid=(group,),
        scratch=[lines, pltpu.VMEM((seq_len, 3 * head_cols), BF)],
    )
    bias_sums = jnp.sum(bias_sums, axis=(0, 1))
    for n, i, part in held:
        came = send(i, tie(part, lin_own))
        batch_adds[n][parent(i)].append(came)
        later_came.append(came)
    later_came = [came for came in later_came if came is not None]
    both = merge(*map(half, terms), [])
    out_sum = collect(out_both, [attn_grad[0]])
    in_grad = tie(collect(both, [out_sum]), *later_came[2:3])
    attn_kinds = [
        (seq_in, [[half(lin_own), half(lin_sib)]]),
        ([half(h) for h in attn_grad], [mixed]),
    ]
    attn_adds = [[] for _ in range(far)]
    parts, attn_sent = [], []
    for n, i in enumerate(wide):
        after = (parts if attn_adds[i] else [both] + parts) if n else []
        part = block_grad(i, attn_kinds, [(v, 0) for v in attn_adds[i]], after)
        parts.append(part)
        attn_sent.append(send(i, part))
        attn_adds[parent(i)].append(attn_sent[-1])
    token_grad = from_rel(resid_grad + norm_back(in_grad, normed_one, inv_one, gains[0]))

    def sum_all(array):
        array = array + sibling(array)
        yield sum((swap(array, m) for m in masks[1:]), array)

    def far_sum(array):
        for at in range(0, len(far_bits), 2):
            pair = [1 << b for b in far_bits[at : at + 2]]
            array = sum((swap(array, m) for m in pair + [sum(pair)][: len(pair) - 1]), array)
        return array

    def both_sums(grad, normed):
        return [jnp.sum(grad * normed, axis=0), jnp.sum(grad, axis=0)]

    norm_sums = jnp.stack(both_sums(in_grad, normed_one) + both_sums(mid_local, normed_two))
    bias_full = lax.dynamic_update_slice(
        jnp.zeros((3, head_cols * group * lax.axis_size("tensor")), F32),
        bias_sums.reshape(3, head_cols),
        (jnp.int32(0), (core * group + rank) * head_cols),
    )
    sums = list(sum_all(jnp.concatenate([from_rel(norm_sums), bias_full])))
    sums.append(far_sum(sums[0]))
    result = from_rel((resid_two + out_sum).astype(BF))
    adds = [(v, 3 * TILE * b[0]) for b, into in zip(batches, batch_adds) for v in into[0]]
    adds.append((last_came, 0))
    mlp_after = parts
    mlp_mine = block_grad(0, all_kinds, adds, mlp_after)
    attn_after = sums[1:] + [result]
    attn_mine = block_grad(0, attn_kinds, [(v, 0) for v in attn_adds[0]], attn_after)
    mlp_came = exchange(tie(mlp_mine, in_grad, out_sum))
    attn_came = exchange(tie(attn_mine, mlp_came))
    gate_up_grad, down_grad = finish(
        finish_mlp_kernel, [mlp_came], (gate_up_weight.shape, down_weight.shape)
    )
    qkv_grad, out_w_grad = finish(
        finish_attn_kernel, [attn_came], (qkv_weight.shape, out_weight.shape)
    )
    sums = sums[-1]
    return (
        result,
        token_grad,
        sums[0],
        sums[1],
        qkv_grad,
        sums[4:],
        out_w_grad,
        sums[2],
        sums[3],
        gate_up_grad,
        down_grad,
    )


def solution(mesh):
    return jax.shard_map(
        on_device,
        mesh=mesh,
        in_specs=(
            P(("dp", "tensor"), None),
            P("dp"),
            P(),
            P(),
            P(None, "dp", "tensor"),
            P(None, "tensor"),
            P("tensor", "dp"),
            P(),
            P(),
            P(None, "dp", "tensor"),
            P("tensor", "dp"),
            P(("dp", "tensor"), None),
        ),
        out_specs=(
            P(("dp", "tensor"), None),
            P(("dp", "tensor"), None),
            P(),
            P(),
            P(None, "dp", "tensor"),
            P(),
            P("tensor", "dp"),
            P(),
            P(),
            P(None, "dp", "tensor"),
            P("tensor", "dp"),
        ),
        check_vma=False,
    )
```

```python
import functools

import jax
import jax.numpy as jnp
from jax import lax
from jax.experimental import pallas as pl
from jax.experimental.pallas import tpu as pltpu
from jax.sharding import PartitionSpec as P

HD = 64
ROT = 16
LANES = 128

norm_eps = 1e-05
rope_base = 10000.0
score_scale = 0.125
masked_score = -1e30

GROUP_BITS = (1, 2)
BF = jnp.bfloat16
F32 = jnp.float32
VMEM_LIMIT = 60 * 1024 * 1024


def norm_parts(values, gain, shift):
    row_mean = jnp.mean(values, axis=-1, keepdims=True)
    centred = values - row_mean
    inv_std = lax.rsqrt(jnp.mean(centred * centred, axis=-1, keepdims=True) + norm_eps)
    normed = centred * inv_std
    return (normed * gain + shift, normed, inv_std)


def norm_back(incoming, normed, inv_std, gain):
    scaled = incoming * gain
    adjusted = (
        scaled
        - jnp.mean(scaled, axis=-1, keepdims=True)
        - normed * jnp.mean(scaled * normed, axis=-1, keepdims=True)
    )
    return adjusted * inv_std


def dot(a, b, a_dim, b_dim):
    return lax.dot_general(
        a, b, (((a_dim,), (b_dim,)), ((), ())), preferred_element_type=F32
    )


def whole(shape, once=False):
    zeros = (0,) * len(shape)
    return pl.BlockSpec(
        shape, lambda *_: zeros, pipeline_mode=pl.Buffered(buffer_count=1) if once else None
    )


def each(shape):
    zeros = (0,) * (len(shape) - 1)
    return pl.BlockSpec((None,) + shape[1:], lambda k, *_: (k,) + zeros)


LONG, SHORT = 30, 0


def call(
    kernel, ins, out_shapes, flops, in_specs=None, out_specs=None, grid=(1,), scratch=(), cost=LONG
):
    moved = cost * sum(v.size * v.dtype.itemsize for v in [*ins, *out_shapes])
    return pl.pallas_call(
        kernel,
        grid=grid,
        in_specs=in_specs or [whole(v.shape) for v in ins],
        out_specs=out_specs or [whole(s.shape) for s in out_shapes],
        out_shape=list(out_shapes),
        scratch_shapes=list(scratch),
        compiler_params=pltpu.CompilerParams(vmem_limit_bytes=VMEM_LIMIT),
        cost_estimate=pl.CostEstimate(flops=cost * flops, bytes_accessed=moved, transcendentals=0),
    )(*ins)


def shaped(shape, dtype):
    return jax.ShapeDtypeStruct(shape, dtype)


def deal(cols, group):
    full = cols // (LANES * group) * LANES
    share = (cols - full * group) // group
    return full, share


def pack_attn_kernel(group, qkv_ref, out_ref, sent_ref):
    cols = qkv_ref.shape[2] // group
    block = qkv_ref.shape[1]
    for k in range(group):
        at, here = slice(k * cols, (k + 1) * cols), slice(k * block, (k + 1) * block)
        for j in range(3):
            sent_ref[here, j * cols : (j + 1) * cols] = qkv_ref[j, :, at]
        sent_ref[here, 3 * cols :] = out_ref[at, :].T


TILE = 2 * LANES


def column(j, at):
    return at // TILE * 3 * TILE + j * TILE + at % TILE


def pack_mlp_kernel(group, gate_up_ref, down_ref, sent_ref):
    full, share = deal(gate_up_ref.shape[2], group)
    block = gate_up_ref.shape[1]
    per = LANES // share
    lane = lax.broadcasted_iota(jnp.int32, (1, LANES), 1) // share
    for k in range(group):
        here = slice(k * block, (k + 1) * block)
        for at in range(0, full + LANES, LANES):
            own = at < full
            start = k * full + at if own else group * full + k // per * LANES
            take = slice(start, start + LANES)
            for j in range(3):
                value = gate_up_ref[j, :, take] if j < 2 else down_ref[take, :].T
                if not own:
                    value = jnp.where(lane == k % per, value, 0).astype(BF)
                to = column(j, at)
                sent_ref[here, to : to + LANES] = value


def finish_mlp_kernel(group, *refs):
    got, gate_up_ref, down_ref = refs
    full, share = deal(gate_up_ref.shape[2], group)
    block = gate_up_ref.shape[1]
    per = LANES // share

    def taken(k, j, at):
        to = column(j, at)
        return got[k * block : (k + 1) * block, to : to + LANES].astype(F32)

    for j in range(3):
        for at in range(0, full + LANES, LANES):
            own = at < full
            for k in range(0, group, 1 if own else per):
                start = k * full + at if own else group * full + k // per * LANES
                take = slice(start, start + LANES)
                value = sum(taken(k + i, j, at) for i in range(1 if own else per))
                if j < 2:
                    gate_up_ref[j, :, take] = value
                else:
                    down_ref[take, :] = value.T


def finish_attn_kernel(group, got_ref, qkv_ref, out_ref):
    cols = qkv_ref.shape[2] // group
    block = qkv_ref.shape[1]
    for k in range(group):
        here, at = slice(k * block, (k + 1) * block), slice(k * cols, (k + 1) * cols)
        for j in range(3):
            qkv_ref[j, :, at] = got_ref[here, j * cols : (j + 1) * cols].astype(F32)
        out_ref[at, :] = got_ref[here, 3 * cols :].astype(F32).T


def spans(weights):
    at = 0
    for w in weights:
        yield slice(at, at + w.shape[0]), w
        at += w.shape[0]


def turn(value, tables, sign):
    cosine, lead, tail = tables
    ahead = pltpu.roll(value, LANES - ROT // 2, 1)
    behind = pltpu.roll(value, ROT // 2, 1)
    return value * cosine + (ahead * lead + behind * tail) * sign


def soft(left, right, mask, axis):
    scores = dot(left, right, 1, 1) * score_scale + mask
    weights = jnp.exp(scores - jnp.max(scores, axis=axis, keepdims=True))
    return weights * (1.0 / jnp.sum(weights, axis=axis, keepdims=True))


def own_head(half):
    return lax.broadcasted_iota(jnp.int32, (1, LANES), 1) // HD == half


def attend_kernel(far, own_ref, sib_ref, bias_ref, mask_ref, cos_ref, lead_ref, tail_ref, *refs):
    weights, refs = refs[:far], refs[far:]
    qkv_ref, mixed_own, mixed_sib, mine_ref, other_ref, lines, mixed_ref = refs
    rows = mine_ref.shape[0]
    lines[:rows] = own_ref[...]
    lines[rows:] = sib_ref[...]
    cols = mixed_ref.shape[1]
    tables = (cos_ref[...], lead_ref[...], tail_ref[...])
    lin = bias_ref[...]
    for at, w in spans(weights):
        lin = lin + dot(lines[:, at], w[:, : 3 * cols], 1, 0)
    mask = mask_ref[...]
    for i in range(cols // LANES):
        at = [slice(j * cols + i * LANES, j * cols + (i + 1) * LANES) for j in range(3)]
        queries = turn(lin[:, at[0]], tables, 1.0).astype(BF)
        keys = turn(lin[:, at[1]], tables, 1.0).astype(BF)
        values = lin[:, at[2]].astype(BF)
        qkv_ref[:, at[0]] = queries
        qkv_ref[:, at[1]] = keys
        qkv_ref[:, at[2]] = values
        mixed = None
        for half in range(LANES // HD):
            here = own_head(half)
            probs = soft(jnp.where(here, queries, 0).astype(BF), keys, mask, 1).astype(BF)
            part = dot(probs, values, 1, 0)
            mixed = part if mixed is None else jnp.where(here, part, mixed)
        mixed_ref[:, i * LANES : (i + 1) * LANES] = mixed.astype(BF)
    mixed_own[...] = mixed_ref[:rows]
    mixed_sib[...] = mixed_ref[rows:]
    for at, w in spans(weights):
        term = dot(mixed_ref[...], w[:, 3 * cols :], 1, 1)
        mine_ref[:, at] = term[:rows].astype(BF)
        other_ref[:, at] = term[rows:].astype(BF)


def attend_back_kernel(far, own_ref, sib_ref, qkv_ref, mask_ref, cos_ref, lead_ref, tail_ref, *refs):
    weights, refs = refs[:far], refs[far:]
    lin_own, lin_sib, sums_ref, mine_ref, other_ref, lines, lin_ref = refs
    rows = own_ref.shape[0]
    lines[:rows] = own_ref[...]
    lines[rows:] = sib_ref[...]
    cols = qkv_ref.shape[1] // 3
    tables = (cos_ref[...], lead_ref[...], tail_ref[...])
    mixed_grad = sum(dot(lines[:, at], w[:, 3 * cols :], 1, 0) for at, w in spans(weights))
    mixed_grad = mixed_grad.astype(BF)
    mask = mask_ref[...]
    for i in range(cols // LANES):
        at = [slice(j * cols + i * LANES, j * cols + (i + 1) * LANES) for j in range(3)]
        queries, keys, values = (qkv_ref[:, a] for a in at)
        grad = mixed_grad[:, i * LANES : (i + 1) * LANES]
        found = [None] * 3
        for half in range(LANES // HD):
            here = own_head(half)
            probs = soft(keys, jnp.where(here, queries, 0).astype(BF), mask, 0)
            value_grad = dot(probs.astype(BF), grad, 1, 0)
            prob_grad = dot(values, jnp.where(here, grad, 0).astype(BF), 1, 1)
            score_grad = (
                probs * (prob_grad - jnp.sum(probs * prob_grad, axis=0, keepdims=True))
            ).astype(BF)
            query_grad = dot(score_grad, keys, 0, 0)
            key_grad = dot(score_grad, queries, 1, 0)
            parts = (query_grad, key_grad, value_grad)
            found = [p if f is None else jnp.where(here, p, f) for p, f in zip(parts, found)]
        lin_ref[:, at[0]] = turn(found[0] * score_scale, tables, -1.0).astype(BF)
        lin_ref[:, at[1]] = turn(found[1] * score_scale, tables, -1.0).astype(BF)
        lin_ref[:, at[2]] = found[2].astype(BF)
    lin_own[...] = lin_ref[:rows]
    lin_sib[...] = lin_ref[rows:]
    sums_ref[...] = jnp.sum(lin_ref[...].astype(F32), axis=0, keepdims=True)
    for at, w in spans(weights):
        term = dot(lin_ref[...], w[:, : 3 * cols], 1, 1)
        mine_ref[:, at] = term[:rows].astype(BF)
        other_ref[:, at] = term[rows:].astype(BF)


def mlp_kernel(far, tiles, first, *refs):
    lines, grads, refs = refs[:2], refs[2:4], refs[4:]
    before, refs = (None, refs) if first else (refs[:2], refs[2:])
    weights, refs = refs[: far * tiles], refs[far * tiles :]
    found, sums, (held, held_grad) = refs[: 4 * tiles], refs[-4:-2], refs[-2:]
    rows = lines[0].shape[0]
    for half in range(2):
        here = slice(half * rows, (half + 1) * rows)
        held[here] = lines[half][...]
        held_grad[here] = grads[half][...]
    inner = []
    for t in range(tiles):
        mine = weights[t * far : (t + 1) * far]
        gate_up = sum(dot(held[:, at], w[:, : 2 * TILE], 1, 0) for at, w in spans(mine))
        hidden_grad = sum(dot(held_grad[:, at], w[:, 2 * TILE :], 1, 0) for at, w in spans(mine))
        gate_pre, up_values = gate_up[:, :TILE], gate_up[:, TILE:]
        gate_sig = jax.nn.sigmoid(gate_pre)
        smooth = gate_pre * gate_sig
        gate_grad = hidden_grad * up_values * gate_sig * (1.0 + gate_pre * (1.0 - gate_sig))
        hidden = (smooth * up_values).astype(BF)
        pair = jnp.concatenate([gate_grad.astype(BF), (hidden_grad * smooth).astype(BF)], axis=1)
        for half in range(2):
            here = slice(half * rows, (half + 1) * rows)
            found[4 * t + half][...] = pair[here]
            found[4 * t + 2 + half][...] = hidden[here]
        inner.append(pair)
    for p, (at, _) in enumerate(spans(weights[:far])):
        term = sum(
            dot(pair, weights[t * far + p][:, : 2 * TILE], 1, 1) for t, pair in enumerate(inner)
        )
        for half in range(2):
            part = term[half * rows : (half + 1) * rows]
            if not first:
                part = part + before[half][:, at]
            sums[half][:, at] = part.astype(sums[half].dtype)


def mlp_out_kernel(far, tiles, *refs):
    hiddens, refs = refs[: 2 * tiles], refs[2 * tiles :]
    weights, outs = refs[: far * tiles], refs[far * tiles :]
    for half in range(2):
        for p, (at, _) in enumerate(spans(weights[:far])):
            term = sum(
                dot(hiddens[2 * t + half][...], weights[t * far + p][...], 1, 1)
                for t in range(tiles)
            )
            outs[half][:, at] = term.astype(outs[half].dtype)


def grad_kernel(kinds, adds, *refs):
    lefts, rights = [], []
    at = 0
    for count in kinds:
        lefts.append(refs[at : at + 2])
        rights.append([refs[at + 2 + 2 * c : at + 4 + 2 * c] for c in range(count)])
        at += 2 + 2 * count
    more, out = refs[at : at + len(adds)], refs[-1]
    start = 0
    for left, columns in zip(lefts, rights):
        for right in columns:
            here = slice(start, start + right[0].shape[1])
            start = here.stop
            total = sum(dot(a[...], b[...], 0, 0) for a, b in zip(left, right))
            for extra, first in zip(more, adds):
                if first <= here.start < first + extra.shape[1]:
                    total = total + extra[:, here.start - first : here.stop - first].astype(F32)
            out[:, here] = total.astype(BF)


def copies_kernel(local_ref, out_ref):
    for k in range(out_ref.shape[0]):
        out_ref[k] = local_ref[...]


def on_device(
    tokens,
    segment_ids,
    ln1_gain,
    ln1_bias,
    qkv_weight,
    qkv_bias,
    out_weight,
    ln2_gain,
    ln2_bias,
    gate_up_weight,
    down_weight,
    out_grad,
):
    dp_size = lax.axis_size("dp")
    bits = dp_size.bit_length() - 1
    me = lax.axis_index("dp")
    core = lax.axis_index("tensor")
    rows, width = tokens.shape
    seq_len = segment_ids.shape[0]
    group = 1 << len(GROUP_BITS)
    far_bits = [b for b in reversed(range(bits)) if b not in GROUP_BITS]
    masks = [
        sum(1 << b for i, b in enumerate(GROUP_BITS) if (k >> i) & 1) for k in range(group)
    ]
    my_bit = [(me >> b) & 1 for b in range(bits)]
    rank = sum(my_bit[b] << i for i, b in enumerate(GROUP_BITS))
    heads = qkv_bias.shape[1] // HD // group
    head_cols = heads * HD
    hidden_cols = deal(down_weight.shape[0], group)[0] + LANES

    def swap(array, mask):
        if mask == 0:
            return array
        return lax.ppermute(array, "dp", [(d, d ^ mask) for d in range(dp_size)])

    def sibling(array):
        return lax.ppermute(array, "tensor", [(0, 1), (1, 0)])

    order = [bits - 1 - b for b in reversed(far_bits)]
    order += [bits - 1 - b for b in reversed(GROUP_BITS)]

    def swapped(array, axis, bit):
        low, high = jnp.split(array, 2, axis)
        low, high = jnp.where(bit == 1, high, low), jnp.where(bit == 1, low, high)
        return jnp.concatenate([low, high], axis)

    def to_rel(array):
        lead = array.ndim - 1
        cut = array.reshape(array.shape[:-1] + (2,) * bits + (width // dp_size,))
        cut = cut.transpose(list(range(lead)) + [lead + o for o in order] + [lead + bits])
        for i, b in enumerate(reversed(far_bits)):
            cut = swapped(cut, lead + i, my_bit[b])
        return cut.reshape(array.shape)

    def from_rel(array):
        lead = array.ndim - 1
        cut = array.reshape(array.shape[:-1] + (2,) * bits + (width // dp_size,))
        for i, b in enumerate(reversed(far_bits)):
            cut = swapped(cut, lead + i, my_bit[b])
        back = [order.index(i) for i in range(bits)]
        cut = cut.transpose(list(range(lead)) + [lead + o for o in back] + [lead + bits])
        return cut.reshape(array.shape)

    block = width // dp_size
    shard_rows = group * block
    far = 1 << len(far_bits)
    bands = [
        [d for d in range(dp_size) if all((d ^ first) >> b & 1 == 0 for b in far_bits)]
        for first in range(dp_size)
        if all(first >> b & 1 == 0 for b in GROUP_BITS)
    ]

    def exchange(rows_by_rank):
        return lax.all_to_all(rows_by_rank, "dp", 0, 0, axis_index_groups=bands, tiled=True)

    def tie(value, *after):
        return lax.optimization_barrier((value, *after))[0]

    def pack(kernel, ins, cols):
        return call(
            functools.partial(kernel, group), ins, [shaped((shard_rows, cols), BF)], 0
        )[0]

    def gather(shard, after=(), after_own=()):
        pieces = [shard]
        for n, b in enumerate(far_bits):
            own = tie(shard, *(after_own if n else after))
            pieces = pieces + [swap(p, 1 << b) for p in [own] + pieces[1:]]
        return pieces

    def copies(local):
        return jnp.broadcast_to(local, (group,) + local.shape)

    def spread(copied, after=(), then=()):
        mine = exchange(tie(copied, *after))
        return mine, sibling(tie(mine, *then))

    def half(array):
        return array.reshape((-1,) + array.shape[2:])

    def by_block(array):
        return array.reshape((group, -1) + array.shape[1:])

    def merge(mine, other, after=()):
        other = sibling(tie(other, *after))
        return (by_block(mine).astype(F32) + by_block(other).astype(F32)).astype(BF)

    def collect(both, after=()):
        return jnp.sum(exchange(tie(both, *after)).astype(F32), axis=0)

    wide = sorted(range(1, far), key=lambda i: (-i.bit_length(), -i))

    def below(i):
        bits_left = range(i.bit_length(), len(far_bits))
        return [c for b in bits_left for c in below(i | 1 << b) + [i | 1 << b]]

    def block_grad(i, kinds, adds, after=(), cost=LONG):
        cols = sum(c[0].shape[1] for _, sets in kinds for c in sets)
        steps = 2 if shard_rows % (2 * LANES) == 0 else 1
        depth = shard_rows // steps
        ins, specs = [], []
        for left, sets in kinds:
            ins += left
            specs += [pl.BlockSpec((v.shape[0], depth), lambda s: (0, steps * i + s)) for v in left]
            for s in sets:
                ins += s
                specs += [whole(v.shape) for v in s]
        ins += [v for v, _ in adds]
        specs += [pl.BlockSpec((depth, v.shape[1]), lambda s: (s, 0)) for v, _ in adds]
        ins[0] = tie(ins[0], *after)
        return call(
            functools.partial(grad_kernel, [len(s) for _, s in kinds], [at for _, at in adds]),
            ins,
            [shaped((shard_rows, cols), BF)],
            2 * group * seq_len * shard_rows * cols,
            in_specs=specs,
            out_specs=[pl.BlockSpec((depth, cols), lambda s: (s, 0))],
            grid=(steps,),
            cost=cost,
        )[0]

    def send(i, part):
        return swap(part, 1 << far_bits[i.bit_length() - 1])

    def parent(i):
        return i ^ 1 << i.bit_length() - 1

    def finish(kernel, came, shapes):
        return call(functools.partial(kernel, group), came, [shaped(s, F32) for s in shapes], 0)

    gains = to_rel(jnp.stack([ln1_gain, ln1_bias, ln2_gain, ln2_bias]))
    resid = to_rel(tokens).astype(F32)
    normed_in, normed_one, inv_one = norm_parts(resid, gains[0], gains[1])
    seq_local = normed_in.astype(BF)
    attn_pack = pack(pack_attn_kernel, [qkv_weight, out_weight], 4 * head_cols)
    attn_shard = exchange(attn_pack)
    segs = jnp.stack([swap(tie(segment_ids, attn_pack), m) for m in masks])
    segs = segs.reshape((2,) * len(GROUP_BITS) + segs.shape[1:])
    for i, b in enumerate(reversed(GROUP_BITS)):
        segs = swapped(segs, i, my_bit[b])
    segs = segs.reshape(group, seq_len)
    mlp_pack = pack(pack_mlp_kernel, [tie(gate_up_weight, attn_shard), down_weight], 3 * hidden_cols)
    mlp_shard = exchange(tie(mlp_pack, attn_shard))
    w_attn = gather(attn_shard)
    tiles = hidden_cols // TILE
    segs = tie(segs, w_attn[2])
    segs = jnp.where(core == 1, jnp.roll(segs, rows, axis=1), segs)
    index = jnp.arange(seq_len, dtype=jnp.int32)
    index = jnp.where(core == 1, jnp.roll(index, rows), index)
    spots = index - jnp.sum(segs[:, None, :] < segs[:, :, None], axis=2, dtype=jnp.int32)
    allowed = (segs[:, :, None] == segs[:, None, :]) & (index[None, :] <= index[:, None])
    mask = jnp.where(allowed, 0.0, masked_score).astype(F32)
    allowed_back = (segs[:, :, None] == segs[:, None, :]) & (index[None, :] >= index[:, None])
    mask_back = jnp.where(allowed_back, 0.0, masked_score).astype(F32)
    dim = jnp.arange(LANES, dtype=jnp.int32) % HD
    pair = (dim % (ROT // 2)).astype(F32)
    speed = jnp.where(dim < ROT, rope_base ** (-2.0 * pair / ROT), 0.0)
    angles = spots.astype(F32)[..., None] * speed
    cosine, sine = jnp.cos(angles), jnp.sin(angles)
    lead = jnp.where(dim < ROT // 2, -sine, 0.0)
    tail = jnp.where((dim >= ROT // 2) & (dim < ROT), sine, 0.0)

    w_mlp = []
    after, after_own = [w_attn[1]], [w_attn[-1]]
    for t in range(tiles):
        shard = mlp_shard[:, t * 3 * TILE : (t + 1) * 3 * TILE]
        w_mlp.append(gather(shard, after, after_own))
        after, after_own = [w_mlp[t][1]], [w_mlp[t][2]]
    grad_local = to_rel(tie(out_grad, w_attn[2]))
    grad_copies = copies(grad_local)
    heard = spread(
        tie(copies(seq_local), grad_copies, cosine, lead, tail, mask),
        [mlp_shard] + w_attn[1:2] + w_attn[2:3],
        w_attn[3:] + w_mlp[0][1:2],
    )
    seq_in = [half(h) for h in heard]
    grad_rows = spread(grad_copies, [heard[0]])

    bias = lax.dynamic_slice_in_dim(qkv_bias, rank * head_cols, head_cols, 1).reshape(1, -1)
    facts = [mask, cosine, lead, tail]
    lines = pltpu.VMEM((seq_len, width), BF)
    mine, other = shaped((group * rows, width), F32), shaped((group * rows, width), BF)
    term3 = shaped((group, rows, width), BF)
    qkv_shape = shaped((group, seq_len, 3 * head_cols), BF)
    mixed_shape = shaped((group, rows, head_cols), BF)
    lin_shape = shaped((group, rows, 3 * head_cols), BF)
    attn_flops = 2 * group * seq_len * width * 4 * head_cols

    ins = [*heard, bias] + facts + w_attn
    outs = [qkv_shape, mixed_shape, mixed_shape, term3, term3]
    qkv, mixed_own, mixed_sib, *terms = call(
        functools.partial(attend_kernel, len(w_attn)),
        ins,
        outs,
        attn_flops,
        in_specs=[each(v.shape) for v in heard]
        + [whole(bias.shape)]
        + [each(v.shape) for v in facts]
        + [whole(v.shape) for v in w_attn],
        out_specs=[each(v.shape) for v in outs],
        grid=(group,),
        scratch=[lines, pltpu.VMEM((seq_len, head_cols), BF)],
    )
    mixed = [half(mixed_own), half(mixed_sib)]
    both = merge(*map(half, terms), w_mlp[0][2:3])
    attn_sum = collect(both, [grad_rows[0]])
    resid_two = resid + tie(
        attn_sum, *w_mlp[0][3:], *w_mlp[1][1:2], *w_mlp[1][2:3]
    )
    normed_mid, normed_two, inv_two = norm_parts(resid_two, gains[2], gains[3])
    seq_mid = [half(h) for h in spread(copies(normed_mid.astype(BF)), (), w_mlp[1][3:] + w_mlp[2][1:2] + w_mlp[2][2:3])]
    grad_rows = [half(h) for h in grad_rows]

    row_spec = pl.BlockSpec((rows, width), lambda k: (k, 0))
    pair_spec, hidden_spec = (pl.BlockSpec((rows, n * TILE), lambda k: (k, 0)) for n in (2, 1))
    pair_shape, hidden_shape = (shaped((group * rows, n * TILE), BF) for n in (2, 1))
    weights = [[w for w in [mlp_shard] + w_mlp[t][1:]] for t in range(tiles)]
    inner, mid = [], []
    for batch in (range(tiles - 1), range(tiles - 1, tiles)):
        ins = [*seq_mid, *grad_rows] + mid
        final = batch[-1] == tiles - 1
        *found, mid_own, mid_sib = call(
            functools.partial(mlp_kernel, far, len(batch), not mid),
            ins + [w for t in batch for w in weights[t]],
            ([pair_shape] * 2 + [hidden_shape] * 2) * len(batch) + [other if final else mine] * 2,
            10 * group * seq_len * width * TILE * len(batch),
            in_specs=[row_spec] * len(ins)
            + [
                pl.BlockSpec((w.shape[0], 3 * TILE), lambda *_, t=0 if n else t: (0, t))
                for t in batch
                for n, w in enumerate(weights[t])
            ],
            out_specs=([pair_spec] * 2 + [hidden_spec] * 2) * len(batch) + [row_spec] * 2,
            grid=(group,),
            scratch=[lines, lines],
        )
        inner += found
        mid = [mid_own, mid_sib]
    weights = [w for ws in weights for w in ws]
    hiddens = [inner[4 * t + 2 : 4 * t + 4] for t in range(tiles)]
    tile_kinds = [
        [(seq_mid, [inner[4 * t : 4 * t + 2]]), (grad_rows, [hiddens[t]])] for t in range(tiles)
    ]
    all_kinds = [kind for kinds in tile_kinds for kind in kinds]
    both = merge(mid_own, mid_sib)

    last = far // 2
    batches = [range(t, t + 1) for t in range(tiles)]
    batch_kinds = [[kind for t in batch for kind in tile_kinds[t]] for batch in batches]
    batch_adds = [[[] for _ in range(far)] for _ in batches]
    first_parts, first_came, later, later_came, held = [], [], [], [], []

    def batch_step(n, i, after):
        part = block_grad(i, batch_kinds[n], [(v, 0) for v in batch_adds[n][i]], after)
        if i == 1 and n >= 2:
            held.append((n, i, part))
            return part, None
        came = send(i, part)
        batch_adds[n][parent(i)].append(came)
        return part, came

    steps = [i for i in below(0) if i != last]
    for n in range(len(batches)):
        part, came = batch_step(n, steps[0], [both] + first_parts if n else [])
        first_parts.append(part)
        first_came.append(came)
    last_part = block_grad(last, all_kinds, [], first_parts, cost=LONG)
    last_came = send(last, last_part)
    mid_local = tie(collect(both), last_part, *first_came[:1])
    resid_grad = grad_local.astype(F32) + norm_back(mid_local, normed_two, inv_two, gains[2])
    resid_back = resid_grad.astype(BF)
    copied = copies(resid_back)
    for i in steps[1:]:
        for n in range(len(batches)):
            part, came = batch_step(n, i, [copied] + later)
            later.append(part)
            later_came.append(came)
    out_ins = [h for pair in hiddens for h in pair]
    out_ins[0] = tie(out_ins[0], copied)
    out_terms = call(
        functools.partial(mlp_out_kernel, far, tiles),
        out_ins + weights,
        [other, other],
        2 * group * seq_len * width * hidden_cols,
        in_specs=[whole(v.shape) for v in out_ins]
        + [
            pl.BlockSpec((w.shape[0], TILE), lambda *_, t=3 * (n // far) if n % far == 0 else 0: (0, t + 2))
            for n, w in enumerate(weights)
        ],
        cost=SHORT,
    )
    out_both = merge(*out_terms)
    attn_grad = spread(copied, [], [out_both] + later + later_came[:1])
    ins = [*attn_grad, qkv, mask_back] + facts[1:] + w_attn
    outs = [lin_shape, lin_shape, shaped((group, 1, 3 * head_cols), F32), term3, term3]
    lin_own, lin_sib, bias_sums, *terms = call(
        functools.partial(attend_back_kernel, len(w_attn)),
        ins,
        outs,
        attn_flops,
        in_specs=[each(v.shape) for v in ins[: 3 + len(facts)]] + [whole(v.shape) for v in w_attn],
        out_specs=[each(v.shape) for v in outs],
        grid=(group,),
        scratch=[lines, pltpu.VMEM((seq_len, 3 * head_cols), BF)],
    )
    bias_sums = jnp.sum(bias_sums, axis=(0, 1))
    for n, i, part in held:
        came = send(i, tie(part, lin_own))
        batch_adds[n][parent(i)].append(came)
        later_came.append(came)
    later_came = [came for came in later_came if came is not None]
    both = merge(*map(half, terms), [])
    out_sum = collect(out_both, [attn_grad[0]])
    in_grad = tie(collect(both, [out_sum]), *later_came[2:3])
    attn_kinds = [
        (seq_in, [[half(lin_own), half(lin_sib)]]),
        ([half(h) for h in attn_grad], [mixed]),
    ]
    attn_adds = [[] for _ in range(far)]
    parts, attn_sent = [], []
    for n, i in enumerate(wide):
        after = (parts if attn_adds[i] else [both] + parts) if n else []
        part = block_grad(i, attn_kinds, [(v, 0) for v in attn_adds[i]], after)
        parts.append(part)
        attn_sent.append(send(i, part))
        attn_adds[parent(i)].append(attn_sent[-1])
    token_grad = from_rel(resid_grad + norm_back(in_grad, normed_one, inv_one, gains[0]))

    def sum_all(array):
        array = array + sibling(array)
        yield sum((swap(array, m) for m in masks[1:]), array)

    def far_sum(array):
        for at in range(0, len(far_bits), 2):
            pair = [1 << b for b in far_bits[at : at + 2]]
            array = sum((swap(array, m) for m in pair + [sum(pair)][: len(pair) - 1]), array)
        return array

    def both_sums(grad, normed):
        return [jnp.sum(grad * normed, axis=0), jnp.sum(grad, axis=0)]

    norm_sums = jnp.stack(both_sums(in_grad, normed_one) + both_sums(mid_local, normed_two))
    bias_full = lax.dynamic_update_slice(
        jnp.zeros((3, head_cols * group * lax.axis_size("tensor")), F32),
        bias_sums.reshape(3, head_cols),
        (jnp.int32(0), (core * group + rank) * head_cols),
    )
    sums = list(sum_all(jnp.concatenate([from_rel(norm_sums), bias_full])))
    sums.append(far_sum(sums[0]))
    result = from_rel((resid_two + out_sum).astype(BF))
    adds = [(v, 3 * TILE * b[0]) for b, into in zip(batches, batch_adds) for v in into[0]]
    adds.append((last_came, 0))
    mlp_after = parts
    mlp_mine = block_grad(0, all_kinds, adds, mlp_after)
    attn_after = sums[1:] + [result]
    attn_mine = block_grad(0, attn_kinds, [(v, 0) for v in attn_adds[0]], attn_after)
    mlp_came = exchange(tie(mlp_mine, in_grad, out_sum))
    attn_came = exchange(tie(attn_mine, mlp_came))
    gate_up_grad, down_grad = finish(
        finish_mlp_kernel, [mlp_came], (gate_up_weight.shape, down_weight.shape)
    )
    qkv_grad, out_w_grad = finish(
        finish_attn_kernel, [attn_came], (qkv_weight.shape, out_weight.shape)
    )
    sums = sums[-1]
    return (
        result,
        token_grad,
        sums[0],
        sums[1],
        qkv_grad,
        sums[4:],
        out_w_grad,
        sums[2],
        sums[3],
        gate_up_grad,
        down_grad,
    )


def solution(mesh):
    return jax.shard_map(
        on_device,
        mesh=mesh,
        in_specs=(
            P(("dp", "tensor"), None),
            P("dp"),
            P(),
            P(),
            P(None, "dp", "tensor"),
            P(None, "tensor"),
            P("tensor", "dp"),
            P(),
            P(),
            P(None, "dp", "tensor"),
            P("tensor", "dp"),
            P(("dp", "tensor"), None),
        ),
        out_specs=(
            P(("dp", "tensor"), None),
            P(("dp", "tensor"), None),
            P(),
            P(),
            P(None, "dp", "tensor"),
            P(),
            P("tensor", "dp"),
            P(),
            P(),
            P(None, "dp", "tensor"),
            P("tensor", "dp"),
        ),
        check_vma=False,
    )
```
